32 devices in a mesh: wide: 8 (over z, core), ctx: 4 (over y, x).
Axes of the slice: x: 2, y: 2, z: 4, core: 2. Of those that a mesh axis runs over, the one named last changes fastest.
Arguments:
- residual: float32 [256, 4096], P('wide', 'ctx'), may hold values from -40 to 40
- grad_out: float32 [256, 4096], P('wide', 'ctx'), may hold values from -6 to 6
- norm_gain: float32 [4096], P('ctx'), may hold values from 0.5 to 1.5
- w_gate: float32 [4096, 14336], P('ctx', 'wide'), may hold values from -0.09375 to 0.09375
- w_up: float32 [4096, 14336], P('ctx', 'wide'), may hold values from -0.09375 to 0.09375
- w_down: float32 [14336, 4096], P('wide', 'ctx'), may hold values from -0.046875 to 0.046875
- w_out: float32 [4096, 4096], P('wide', 'ctx'), may hold values from -0.09375 to 0.09375
- queries: float32 [256, 4096], P('ctx', 'wide'), may hold values from -12 to 12
- attn_out: float32 [256, 4096], P('ctx', 'wide'), may hold values from -3 to 3
- log_sum_exp: float32 [32, 256], P('wide', 'ctx'), as said below
- key_cache: float32 [8, 4096, 128], P('wide', 'ctx'), may hold values from -16 to 16
- value_cache: float32 [8, 4096, 128], P('wide', 'ctx'), may hold values from -6 to 6
Outputs:
- grad_w_gate: float32 [4096, 14336], P('ctx', 'wide')
- grad_w_up: float32 [4096, 14336], P('ctx', 'wide')
- grad_w_down: float32 [14336, 4096], P('wide', 'ctx')
- grad_w_out: float32 [4096, 4096], P('wide', 'ctx')
- grad_resid: float32 [256, 4096], P('wide', 'ctx')
- grad_queries: float32 [256, 4096], P('ctx', 'wide')
The draws below stay inside these ranges and needn't reach their ends.
Inputs may be any that keep to these rules, and one draw needn't show every extreme that they name: `log_sum_exp`: for each head and row, the logarithm of the sum of exp(score) over the positions that the row sees, with score as in the reference program, plus a shift between 0 and 0.2.
All inputs are finite; a program needn't handle non-finite values.
Results may differ from the reference program's by a relative error of at most 0.0003.
Values sent between devices are 32-bit elements; how exact they have to be, the bound alone decides.
No kernel may reach another device: no remote copies, remote signals or barrier semaphores. Data moves between devices by JAX's collectives and lax.ppermute only.
A program may use at most 128 MiB of HBM per device.

```python
import math
import jax
import jax.numpy as jnp
from jax import lax

D = 4096
FF = 14336
QH = 32
KVH = 8
HD = 128
ROWS = 256
SPLIT = 1
CONTEXT = 4096


def joint_draw(key):
    query_key = jax.random.fold_in(key, 101)
    cache_key = jax.random.fold_in(key, 202)
    drawn_queries = jax.random.normal(query_key, (ROWS, QH * HD), jnp.float32)
    drawn_keys = 2.0 * jax.random.normal(cache_key, (KVH * SPLIT, CONTEXT // SPLIT, HD), jnp.float32)
    return (drawn_queries, drawn_keys)


def draw_queries(key, part):
    return joint_draw(key)[0]


def draw_key_cache(key, part):
    return joint_draw(key)[1]


def draw_log_sum_exp(key, part):
    drawn_queries, drawn_keys = joint_draw(key)
    grouped = drawn_keys.reshape(KVH, CONTEXT, HD)
    query_heads = drawn_queries.reshape(ROWS, QH, HD).transpose(1, 0, 2)
    query_pos = CONTEXT - ROWS + jnp.arange(ROWS, dtype=jnp.int32)
    key_pos = jnp.arange(CONTEXT, dtype=jnp.int32)

    def one_head(head_index):
        head_keys = lax.dynamic_index_in_dim(grouped, head_index // (QH // KVH), 0, keepdims=False)
        head_queries = lax.dynamic_index_in_dim(query_heads, head_index, 0, keepdims=False)
        scores = jnp.dot(head_queries, head_keys.T, precision=lax.Precision.HIGHEST) / math.sqrt(HD)
        scores = jnp.where(key_pos[None, :] <= query_pos[:, None], scores, -1e+30)
        return jax.nn.logsumexp(scores, axis=1)
    exact = lax.map(one_head, jnp.arange(QH, dtype=jnp.int32))
    shifted = jax.random.uniform(jax.random.fold_in(key, 303), (QH, ROWS), jnp.float32, 0.0, 0.2)
    return exact + shifted


def draw_residual(key, part):
    base = jax.random.normal(jax.random.fold_in(key, 505), (ROWS, D), jnp.float32)
    rough = jax.random.uniform(jax.random.fold_in(key, 606), (ROWS, D), jnp.float32, 0.7, 1.4)
    column_scale = jnp.exp(jnp.linspace(math.log(0.6), math.log(1.8), D))
    return base * rough * column_scale[None, :]


def block_scale(rng, extent, split, low, largest):
    def one(axis_at, parts):
        steps = jax.random.uniform(jax.random.fold_in(jax.random.fold_in(rng, 6), axis_at), (parts,), jnp.float32, low / len(split), largest / len(split))
        return jnp.repeat(jnp.exp(steps), extent[axis_at] // parts).reshape((-1,) + (1,) * (len(extent) - axis_at - 1))

    factor_of = one(*split[0])
    for cut in split[1:]:
        factor_of = factor_of * one(*cut)
    return factor_of


def bell_draw(own_key, extent, scale, most, pieces=(), held_as=jnp.bfloat16):
    values = scale * jax.random.normal(own_key, extent, jnp.float32)
    if pieces:
        values = values * block_scale(own_key, extent, pieces, -0.22, 0.18)
    return jnp.clip(values, -most, most).astype(held_as)


def setup_inputs(seed: int = 0) -> dict:
    keys = jax.random.split(jax.random.key(seed), 13)
    residual = draw_residual(jax.random.fold_in(keys[12], 71), 0)
    grad_out = bell_draw(keys[1], (ROWS, D), 1.0, 6.0, ((0, 8), (1, 4)), jnp.float32)
    norm_gain = jnp.clip(1.0 + 0.1 * jax.random.normal(keys[2], (D,), jnp.float32), 0.5, 1.5)
    w_gate = bell_draw(keys[3], (D, FF), D ** -0.5, 0.09375, ((0, 4), (1, 8)), jnp.float32)
    w_up = bell_draw(keys[4], (D, FF), D ** -0.5, 0.09375, ((0, 4), (1, 8)), jnp.float32)
    w_down = bell_draw(keys[5], (FF, D), FF ** -0.5, 0.046875, ((0, 8), (1, 4)), jnp.float32)
    w_out = bell_draw(keys[6], (QH * HD, D), D ** -0.5, 0.09375, ((0, 8), (1, 4)), jnp.float32)
    queries = draw_queries(jax.random.fold_in(keys[12], 71), 0)
    attn_out = bell_draw(keys[8], (ROWS, QH * HD), 0.5, 3.0, ((0, 4), (1, 8)), jnp.float32)
    log_sum_exp = draw_log_sum_exp(jax.random.fold_in(keys[12], 71), 0)
    key_cache = draw_key_cache(jax.random.fold_in(keys[12], 71), 0)
    value_cache = bell_draw(keys[11], (KVH * SPLIT, CONTEXT // SPLIT, HD), 1.0, 6.0, ((0, 8), (1, 4)), jnp.float32)
    return {"residual": residual, "grad_out": grad_out, "norm_gain": norm_gain, "w_gate": w_gate, "w_up": w_up, "w_down": w_down, "w_out": w_out, "queries": queries, "attn_out": attn_out, "log_sum_exp": log_sum_exp, "key_cache": key_cache, "value_cache": value_cache}


epsilon = 1e-05
highest = lax.Precision.HIGHEST

def matmul(left, right):
    return jnp.dot(left, right, precision=highest, preferred_element_type=jnp.float32)

def reference(residual, grad_out, norm_gain, w_gate, w_up, w_down, w_out, queries, attn_out, log_sum_exp, key_cache, value_cache):
    inv_rms = lax.rsqrt(lax.optimization_barrier(jnp.mean(residual * residual, axis=1)) + epsilon)
    normed = residual * inv_rms[:, None] * norm_gain[None, :]
    gate_out = matmul(normed, w_gate)
    up_out = matmul(normed, w_up)
    d_hidden = matmul(grad_out, w_down.T)
    sigmoid_gate = jax.nn.sigmoid(gate_out)
    activated = gate_out * sigmoid_gate
    hidden = activated * up_out
    grad_w_down = matmul(hidden.T, grad_out)
    d_up = d_hidden * activated
    d_gate = d_hidden * up_out * sigmoid_gate * (1.0 + gate_out * (1.0 - sigmoid_gate))
    grad_w_gate = matmul(normed.T, d_gate)
    grad_w_up = matmul(normed.T, d_up)
    d_normed = matmul(d_gate, w_gate.T) + matmul(d_up, w_up.T)
    scaled = d_normed * norm_gain[None, :]
    row_dot = lax.optimization_barrier(jnp.sum(residual * scaled, axis=1))
    cubed = inv_rms * inv_rms * inv_rms
    grad_resid = grad_out + inv_rms[:, None] * scaled - residual * (cubed * row_dot / D)[:, None]
    d_attn = matmul(grad_resid, w_out.T)
    grad_w_out = matmul(attn_out.T, grad_resid)
    all_keys = key_cache.reshape(KVH, CONTEXT, HD)
    all_values = value_cache.reshape(KVH, CONTEXT, HD)
    query_heads = queries.reshape(ROWS, QH, HD).transpose(1, 0, 2)
    dout_heads = d_attn.reshape(ROWS, QH, HD).transpose(1, 0, 2)
    output_heads = attn_out.reshape(ROWS, QH, HD).transpose(1, 0, 2)
    delta = lax.optimization_barrier(jnp.sum(dout_heads * output_heads, axis=2))
    scale = 1.0 / HD ** 0.5
    query_pos = CONTEXT - ROWS + jnp.arange(ROWS, dtype=jnp.int32)
    key_pos = jnp.arange(CONTEXT, dtype=jnp.int32)
    visible = key_pos[None, :] <= query_pos[:, None]

    def one_head(head_index):
        group_index = head_index // (QH // KVH)
        head_keys = lax.dynamic_index_in_dim(all_keys, group_index, 0, keepdims=False)
        head_values = lax.dynamic_index_in_dim(all_values, group_index, 0, keepdims=False)
        head_queries = lax.dynamic_index_in_dim(query_heads, head_index, 0, keepdims=False)
        head_dout = lax.dynamic_index_in_dim(dout_heads, head_index, 0, keepdims=False)
        head_lse = lax.dynamic_index_in_dim(log_sum_exp, head_index, 0, keepdims=False)
        head_delta = lax.dynamic_index_in_dim(delta, head_index, 0, keepdims=False)
        scores = matmul(head_queries, head_keys.T) * scale
        probs = jnp.where(visible, jnp.exp(scores - head_lse[:, None]), 0.0)
        dprobs = matmul(head_dout, head_values.T)
        return matmul(probs * (dprobs - head_delta[:, None]), head_keys) * scale
    per_head = lax.map(one_head, jnp.arange(QH, dtype=jnp.int32))
    grad_queries = per_head.transpose(1, 0, 2).reshape(ROWS, QH * HD)
    return (grad_w_gate, grad_w_up, grad_w_down, grad_w_out, grad_resid, grad_queries)
```

```python
import functools
import math

import jax
import jax.numpy as jnp
from jax import lax
from jax.experimental import pallas as pl
from jax.experimental.pallas import tpu as pltpu
from jax.sharding import PartitionSpec as P

KVH = 8
HD = 128


epsilon = 1e-05
highest = lax.Precision.HIGHEST
f32 = jnp.float32
bf16 = jnp.bfloat16
LANES = 128
TILE = 256
VMEM_LIMIT = 16 * 1024 * 1024
VMEM_MOST = 60 * 1024 * 1024
NN = (((1,), (0,)), ((), ()))
NT = (((1,), (1,)), ((), ()))
TN = (((0,), (0,)), ((), ()))


def flip(block, axis, mask):
    count = lax.axis_size(axis)
    return lax.ppermute(block, axis, [(at, at ^ mask) for at in range(count)])


def pieces(values):
    high = values.astype(bf16)
    return high, (values - high.astype(f32)).astype(bf16)


def dot(left, right, dims):
    return lax.dot_general(left, right, dims, preferred_element_type=f32)


def dot3(left, right, dims):
    left_high, left_low = left
    right_high, right_low = right
    return (
        dot(left_high, right_high, dims)
        + dot(left_low, right_high, dims)
        + dot(left_high, right_low, dims)
    )


class Chain:
    def __init__(self):
        self.links = []

    def wait(self, *arrays):
        self.links += arrays


def call(
    name,
    kernel,
    grid,
    in_specs,
    out_specs,
    out_shape,
    scratch=(),
    flops=0,
    moved=0,
    after=None,
    limit=VMEM_LIMIT,
):
    count, waits, outs = len(in_specs), len(after.links), len(out_specs)

    def body(*refs):
        link = refs[count + waits + outs]
        link[...] = jnp.zeros_like(link)
        kernel(*refs[:count], *refs[count + waits : count + waits + outs], *refs[count + waits + outs + 1 :])

    run = pl.pallas_call(
        body,
        name=name,
        grid=grid,
        in_specs=list(in_specs) + [pl.BlockSpec(memory_space=pl.ANY)] * waits,
        out_specs=list(out_specs) + [whole((8, LANES))],
        out_shape=list(out_shape) + [shape_of(8, LANES)],
        scratch_shapes=list(scratch),
        compiler_params=pltpu.CompilerParams(vmem_limit_bytes=limit),
        cost_estimate=pl.CostEstimate(flops=4 * flops, bytes_accessed=4 * moved, transcendentals=0),
    )

    def apply(*operands):
        *results, link = run(*operands, *after.links)
        after.links = [link]
        return results if len(results) > 1 else results[0]

    return apply


def ordered(array, *earlier):
    anywhere = pl.BlockSpec(memory_space=pl.ANY)
    return pl.pallas_call(
        lambda *refs: None,
        name="ordered",
        in_specs=[anywhere] * (1 + len(earlier)),
        out_specs=anywhere,
        out_shape=jax.ShapeDtypeStruct(array.shape, array.dtype),
        input_output_aliases={0: 0},
    )(array, *earlier)


def whole(shape):
    return pl.BlockSpec(shape, lambda *_: (0,) * len(shape))


def shape_of(*shape, dtype=f32):
    return jax.ShapeDtypeStruct(shape, dtype)


def partial_kernel(orders, *refs):
    units = len(orders)
    sources = refs[: 2 * units]
    gain, w_gate, w_up, w_down = refs[2 * units : 2 * units + 4]
    results = refs[2 * units + 4 : -2]
    x_parts, g_parts = refs[-2:]
    step = pl.program_id(0)
    width = gain.shape[1]
    count = results[2].shape[0]
    total = units * count
    hidden = (results[0].shape[1] - LANES) // 3

    @pl.when(step == 0)
    def _():
        for unit, order in enumerate(orders):
            own, far = sources[2 * unit : 2 * unit + 2]
            keep, send, rows = results[3 * unit : 3 * unit + 3]
            cut = count // len(order)
            for at, rel in enumerate(order):
                piece = pl.ds(rel * cut // 2, cut // 2)
                rows[pl.ds(at * cut, cut // 2), :] = own[piece, :]
                rows[pl.ds(at * cut + cut // 2, cut // 2), :] = far[piece, :]
            resid = rows[:, :width]
            squares = jnp.broadcast_to(
                jnp.sum(resid * resid, axis=1, keepdims=True), (count, LANES)
            )
            keep[:, pl.ds(3 * hidden, LANES)] = squares[: count // 2]
            send[:, pl.ds(3 * hidden, LANES)] = squares[count // 2 :]
            gained = resid * gain[...]
            rows[:, :width] = gained
            for parts, values in ((x_parts, gained), (g_parts, rows[:, width:])):
                high, low = pieces(values)
                parts[pl.ds(unit * count, count), :] = high
                parts[pl.ds(total + unit * count, count), :] = low

    at = pl.multiple_of(step * TILE, TILE)
    for section, parts, weight, dims in (
        (0, x_parts, w_gate, NN),
        (1, x_parts, w_up, NN),
        (2, g_parts, w_down, NT),
    ):
        high, low = pieces(weight[...])
        both = dot(parts[...], high, dims)
        value = both[:total] + both[total:] + dot(parts[:total, :], low, dims)
        place = pl.ds(section * hidden + at, TILE)
        for unit in range(units):
            keep, send = results[3 * unit : 3 * unit + 2]
            start = unit * count
            keep[:, place] = value[start : start + count // 2]
            send[:, place] = value[start + count // 2 : start + count]


def partial_sums(orders, sources, gain, w_gate, w_up, w_down, after):
    width, hidden = w_gate.shape
    own_shape = sources[0][0].shape
    count = 2 * own_shape[0]
    total = count * len(orders)
    half = (count // 2, 3 * hidden + LANES)
    both = (count, 2 * width)
    flat = [item for pair in sources for item in pair]
    results = call(
        "partial",
        functools.partial(partial_kernel, orders),
        (hidden // TILE,),
        [whole(own_shape)] * len(flat)
        + [
            whole((1, width)),
            pl.BlockSpec((width, TILE), lambda j: (0, j)),
            pl.BlockSpec((width, TILE), lambda j: (0, j)),
            pl.BlockSpec((TILE, width), lambda j: (j, 0)),
        ],
        [whole(half), whole(half), whole(both)] * len(orders),
        [shape_of(*half), shape_of(*half), shape_of(*both)] * len(orders),
        [pltpu.VMEM((2 * total, width), bf16), pltpu.VMEM((2 * total, width), bf16)],
        flops=18 * total * width * hidden,
        moved=12 * width * hidden,
        after=after,
        limit=VMEM_MOST,
    )(*flat, gain, w_gate, w_up, w_down)
    return [results[3 * unit : 3 * unit + 3] for unit in range(len(orders))]


def fold_kernel(kept, got, keep, send):
    half = keep.shape[0]
    keep[...] = kept[:half, :] + got[:half, :]
    send[...] = kept[half:, :] + got[half:, :]


def fold(kept, got, after):
    rows, columns = kept.shape
    half = (rows // 2, columns)
    return call(
        "fold",
        fold_kernel,
        (1,),
        [whole(kept.shape)] * 2,
        [whole(half)] * 2,
        [shape_of(*half)] * 2,
        flops=rows * columns,
        moved=12 * rows * columns,
        after=after,
    )(kept, got)


def join_kernel(one, other, out):
    out[...] = one[...] + other[...]


def join(one, other, after):
    return call(
        "join",
        join_kernel,
        (1,),
        [whole(one.shape)] * 2,
        [whole(one.shape)],
        [shape_of(*one.shape)],
        moved=12 * one.size,
        after=after,
    )(one, other)


def middle_kernel(width, kept, got, out):
    hidden = (out.shape[1] - LANES) // 3
    gate_at, up_at, down_at = (pl.ds(part * hidden, hidden) for part in range(3))
    rest = pl.ds(3 * hidden, LANES)
    squares = (kept[:, rest] + got[:, rest])[:, :1]
    inv_rms = lax.rsqrt(squares / width + epsilon)
    gate_raw = kept[:, gate_at] + got[:, gate_at]
    up_raw = kept[:, up_at] + got[:, up_at]
    d_hidden = kept[:, down_at] + got[:, down_at]
    gate_out = gate_raw * inv_rms
    up_out = up_raw * inv_rms
    sigmoid_gate = jax.nn.sigmoid(gate_out)
    activated = gate_out * sigmoid_gate
    d_up = d_hidden * activated * inv_rms
    d_gate = d_hidden * up_out * sigmoid_gate * (1.0 + gate_out * (1.0 - sigmoid_gate)) * inv_rms
    out[:, gate_at] = d_gate
    out[:, up_at] = d_up
    out[:, down_at] = activated * up_out
    row_sum = jnp.sum(d_gate * gate_raw + d_up * up_raw, axis=1, keepdims=True)
    out[:, rest] = jnp.broadcast_to(row_sum * (inv_rms * inv_rms / width), (out.shape[0], LANES))


def middle(width, kept, got, after):
    rows, columns = kept.shape
    return call(
        "middle",
        functools.partial(middle_kernel, float(width)),
        (1,),
        [whole(kept.shape)] * 2,
        [whole(kept.shape)],
        [shape_of(rows, columns)],
        flops=20 * rows * columns,
        moved=12 * rows * columns,
        after=after,
    )(kept, got)


def normed_kernel(order, *refs):
    blocks = refs[: len(order)]
    w_gate, w_up, own, far, split, parts = refs[len(order) :]
    step = pl.program_id(0)
    cut = blocks[0].shape[0]
    count = cut * len(order)
    hidden = w_gate.shape[1]
    width = own.shape[1] - LANES

    @pl.when(step == 0)
    def _():
        for at, block in enumerate(blocks):
            high, low = pieces(block[:, : 3 * hidden])
            split[0, pl.ds(at * cut, cut), :] = high
            split[1, pl.ds(at * cut, cut), :] = low
            for section in range(2):
                columns = slice(section * hidden, (section + 1) * hidden)
                parts[section, pl.ds(at * cut, cut), :] = high[:, columns]
                parts[section, pl.ds(count + at * cut, cut), :] = low[:, columns]
            terms = block[:, pl.ds(3 * hidden, LANES)]
            piece = pl.ds(order[at] * cut // 2, cut // 2)
            own[piece, pl.ds(width, LANES)] = terms[: cut // 2]
            far[piece, pl.ds(width, LANES)] = terms[cut // 2 :]

    total = jnp.zeros((count, TILE), f32)
    for section, weight in ((0, w_gate), (1, w_up)):
        high, low = pieces(weight[...])
        both = dot(parts[section], high, NT)
        total += both[:count] + both[count:] + dot(parts[section, :count, :], low, NT)
    place = pl.ds(pl.multiple_of(step * TILE, TILE), TILE)
    for at, rel in enumerate(order):
        piece = pl.ds(rel * cut // 2, cut // 2)
        own[piece, place] = total[at * cut : at * cut + cut // 2]
        far[piece, place] = total[at * cut + cut // 2 : (at + 1) * cut]


def normed_sums(order, blocks, w_gate, w_up, after):
    width, hidden = w_gate.shape
    cut = blocks[0].shape[0]
    count = cut * len(order)
    half = (count // 2, width + LANES)
    weight = pl.BlockSpec((TILE, hidden), lambda j: (j, 0))
    return call(
        "normed",
        functools.partial(normed_kernel, order),
        (width // TILE,),
        [whole(blocks[0].shape)] * len(order) + [weight, weight],
        [whole(half), whole(half), whole((2, count, 3 * hidden))],
        [shape_of(*half), shape_of(*half), shape_of(2, count, 3 * hidden, dtype=bf16)],
        [pltpu.VMEM((2, 2 * count, hidden), bf16)],
        flops=12 * count * width * hidden,
        moved=8 * width * hidden,
        after=after,
    )(*blocks, w_gate, w_up)


def collect_kernel(*refs):
    rows, left, right = refs[:-2], refs[-2], refs[-1]
    width = right.shape[2]
    gained = jnp.concatenate([item[:, :width] for item in rows], axis=0)
    left[0], left[1] = pieces(gained.T)
    right[0], right[1] = pieces(jnp.concatenate([item[:, width:] for item in rows], axis=0))


def collect(rows, after):
    total, width = sum(item.shape[0] for item in rows), rows[0].shape[1] // 2
    return call(
        "collect",
        collect_kernel,
        (1,),
        [whole(item.shape) for item in rows],
        [whole((2, width, total)), whole((2, total, width))],
        [shape_of(2, width, total, dtype=bf16), shape_of(2, total, width, dtype=bf16)],
        moved=16 * total * width,
        after=after,
        limit=VMEM_MOST,
    )(*rows)


def weight_kernel(flipped, rows, *refs):
    splits, out = refs[:-1], refs[-1]
    high = jnp.concatenate([split[0] for split in splits], axis=0)
    low = jnp.concatenate([split[1] for split in splits], axis=0)
    held = (rows[0], rows[1])
    out[...] = dot3((high, low), held, TN) if flipped else dot3(held, (high, low), NN)


def weight_grad(section, rows, splits, hidden, after):
    flipped = section == 2
    width, total = (rows.shape[2], rows.shape[1]) if flipped else rows.shape[1:]
    tiles = hidden // TILE
    if flipped:
        out_spec, out_shape = pl.BlockSpec((TILE, width), lambda j: (j, 0)), (hidden, width)
    else:
        out_spec, out_shape = pl.BlockSpec((width, TILE), lambda j: (0, j)), (width, hidden)
    return call(
        "weight",
        functools.partial(weight_kernel, flipped),
        (tiles,),
        [whole(rows.shape)]
        + [
            pl.BlockSpec((2, split.shape[1], TILE), lambda j: (0, 0, section * tiles + j))
            for split in splits
        ],
        [out_spec],
        [shape_of(*out_shape)],
        flops=6 * total * width * hidden,
        moved=4 * width * hidden,
        after=after,
        limit=VMEM_MOST,
    )(rows, *splits)


def by_head(source, heads):
    return jnp.concatenate([source[:, at * HD : (at + 1) * HD] for at in range(heads)], axis=0)


def probs_kernel(heads, scale, place, first, queries, lse, keys, *refs):
    rest, probs = refs[:-1], refs[-1]
    rows = queries.shape[0]
    query_rows = by_head(queries, heads)
    shift = lse[...]
    row_at = lax.broadcasted_iota(jnp.int32, (heads * rows, 1), 0)
    row_pos = lax.rem(row_at, rows) + first[0]
    for at, source in enumerate((keys,) + rest):
        key_count = source.shape[0]
        for begin in range(0, key_count, TILE):
            scores = lax.dot_general(
                query_rows,
                source[pl.ds(begin, TILE), :],
                NT,
                precision=highest,
                preferred_element_type=f32,
            )
            key_at = lax.broadcasted_iota(jnp.int32, (1, TILE), 1)
            key_pos = key_at + (place[at] * key_count + begin)
            probs[:, pl.ds(at * key_count + begin, TILE)] = jnp.where(
                key_pos <= row_pos, jnp.exp(scores * scale - shift), 0.0
            )


def probs_of(place, first, queries, lse, keys, key_count, after):
    rows, columns = queries.shape
    heads = columns // HD
    scalar = pl.BlockSpec(memory_space=pltpu.SMEM)
    total = (heads * rows, key_count * len(keys))
    return call(
        "probs",
        functools.partial(probs_kernel, heads, 1.0 / math.sqrt(HD)),
        (1,),
        [scalar, scalar, whole(queries.shape), whole(lse.shape)]
        + [pl.BlockSpec((key_count, HD), lambda i: (0, 0))] * len(keys),
        [whole(total)],
        [shape_of(*total)],
        flops=12 * rows * columns * total[1],
        moved=4 * total[0] * total[1],
        after=after,
    )(place, first, queries, lse, *keys)


def attend_kernel(heads, scale, probs, outs, *refs):
    out = refs[-1]
    count = (len(refs) - 1) // 3
    douts, keys, values = refs[:count], refs[count : 2 * count], refs[2 * count : 3 * count]
    rows = outs.shape[0]
    dout = douts[0][...]
    for other in douts[1:]:
        dout = dout + other[...]
    dout_rows = by_head(dout, heads)
    delta = jnp.sum(dout_rows * by_head(outs, heads), axis=1, keepdims=True)
    dout_parts = pieces(dout_rows)
    total = jnp.zeros((heads * rows, HD), f32)
    for at in range(count):
        key_count = keys[at].shape[0]
        for begin in range(0, key_count, TILE):
            part = pl.ds(begin, TILE)
            dprobs = dot3(dout_parts, pieces(values[at][part, :]), NT)
            weights = probs[:, pl.ds(at * key_count + begin, TILE)] * (dprobs - delta)
            total += dot3(pieces(weights), pieces(keys[at][part, :]), NN)
    for head in range(heads):
        out[:, head * HD : (head + 1) * HD] = total[head * rows : (head + 1) * rows] * scale


def attend(probs, outs, douts, keys, values, key_count, after):
    rows, columns = outs.shape
    block = pl.BlockSpec((key_count, HD), lambda i: (0, 0))
    return call(
        "attend",
        functools.partial(attend_kernel, columns // HD, 1.0 / math.sqrt(HD)),
        (1,),
        [whole(probs.shape), whole(outs.shape)]
        + [whole(outs.shape)] * len(douts)
        + [block] * (len(keys) + len(values)),
        [whole(outs.shape)],
        [shape_of(rows, columns)],
        flops=12 * rows * columns * key_count * len(keys),
        moved=4 * (probs.size + 2 * key_count * HD * len(keys)),
        after=after,
    )(probs, outs, *douts, *keys, *values)


def attn_grad_kernel(blocks, place, weight, *refs):
    sources, outs = refs[:blocks], refs[blocks:-2]
    rel_rows, parts = refs[-2:]
    cut = outs[0].shape[0]
    total = cut * len(outs)
    piece = total // blocks

    @pl.when(pl.program_id(0) == 0)
    def _():
        for at, source in enumerate(sources):
            high, low = pieces(source[...])
            start = pl.multiple_of(place[at] * piece, piece)
            rel_rows[pl.ds(start, piece), :] = source[...]
            parts[pl.ds(start, piece), :] = high
            parts[pl.ds(pl.multiple_of(total + start, piece), piece), :] = low

    high, low = pieces(weight[...])
    both = dot(parts[...], high, NT)
    result = both[:total] + both[total:] + dot(parts[:total, :], low, NT)
    for at, out in enumerate(outs):
        out[...] = result[at * cut : (at + 1) * cut]


def attn_grad(place, sources, weight, count, after):
    piece, width = sources[0].shape
    total = piece * len(sources)
    columns = weight.shape[0]
    part = (total // count, columns)
    return call(
        "attn_grad",
        functools.partial(attn_grad_kernel, len(sources)),
        (columns // TILE,),
        [pl.BlockSpec(memory_space=pltpu.SMEM), pl.BlockSpec((TILE, width), lambda j: (j, 0))]
        + [whole(source.shape) for source in sources],
        [pl.BlockSpec((part[0], TILE), lambda j: (0, j))] * count + [whole((total, width))],
        [shape_of(*part)] * count + [shape_of(total, width)],
        [pltpu.VMEM((2 * total, width), bf16)],
        flops=6 * total * width * columns,
        moved=4 * width * columns,
        after=after,
    )(place, weight, *sources)


def out_weight_kernel(*refs):
    outs, (resid, grad) = refs[:-2], refs[-2:]
    rows = resid.shape[0] // len(outs)
    head = pl.ds(pl.multiple_of(pl.program_id(0) * rows, rows), rows)
    left = jnp.concatenate([out[head, :] for out in outs], axis=0)
    grad[...] = dot3(pieces(left), pieces(resid[...]), TN)


def out_weight_grad(outs, resid, heads, after):
    total, width = resid.shape
    return call(
        "out_weight",
        out_weight_kernel,
        (heads,),
        [pl.BlockSpec((heads * total // len(outs), HD), lambda j, at=at: (at, 0)) for _, at in outs]
        + [whole(resid.shape)],
        [pl.BlockSpec((HD, width), lambda j: (j, 0))],
        [shape_of(heads * HD, width)],
        flops=6 * total * width * heads * HD,
        moved=4 * width * heads * HD,
        after=after,
    )(*[item for item, _ in outs], resid)


def arrange_kernel(count, place, resid, grad, out, again):
    rows, width = resid.shape
    cut = rows // count
    for rel in range(count):
        source = pl.ds(pl.multiple_of(place[rel] * cut, cut), cut)
        out[pl.ds(rel * cut, cut), :width] = resid[source, :]
        out[pl.ds(rel * cut, cut), width:] = grad[source, :]
    again[...] = out[...]


def arrange(place, resid, grad, count, after):
    rows, width = resid.shape
    return call(
        "arrange",
        functools.partial(arrange_kernel, count),
        (1,),
        [pl.BlockSpec(memory_space=pltpu.SMEM)] + [whole(resid.shape)] * 2,
        [whole((rows, 2 * width))] * 2,
        [shape_of(rows, 2 * width)] * 2,
        moved=16 * rows * width,
        after=after,
        limit=VMEM_MOST,
    )(place, resid, grad)


def finish_kernel(count, place, rows_rel, gain, *refs):
    parts, out = refs[:-1], refs[-1]
    rows, width = out.shape
    cut = rows // count
    total = parts[0][...]
    for part in parts[1:]:
        total = total + part[...]
    result = (
        rows_rel[:, width:]
        + gain[...] * total[:, :width]
        - rows_rel[:, :width] * total[:, width : width + 1]
    )
    for rel in range(count):
        target = pl.ds(pl.multiple_of(place[rel] * cut, cut), cut)
        out[target, :] = result[rel * cut : (rel + 1) * cut]


def finish(place, rows_rel, gain, parts, count, after):
    rows, width = rows_rel.shape[0], gain.shape[1]
    return call(
        "finish",
        functools.partial(finish_kernel, count),
        (1,),
        [pl.BlockSpec(memory_space=pltpu.SMEM), whole(rows_rel.shape), whole(gain.shape)]
        + [whole(part.shape) for part in parts],
        [whole((rows, width))],
        [shape_of(rows, width)],
        moved=4 * rows * width * (len(parts) + 3),
        after=after,
    )(place, rows_rel, gain, *parts)


def save_kernel(heads, keys, values, outs, saved, kept):
    kept[...] = values[...]
    count = keys.shape[0]
    rows = outs.shape[0]
    saved[pl.ds(0, count), :] = keys[...]
    for head in range(heads):
        saved[pl.ds(count + head * rows, rows), :] = outs[:, head * HD : (head + 1) * HD]


def save(keys, values, outs, after):
    count, rows, columns = keys.shape[0], outs.shape[0], outs.shape[1]
    heads = columns // HD
    total = (count + heads * rows, HD)
    return call(
        "save",
        functools.partial(save_kernel, heads),
        (1,),
        [whole(keys.shape), whole(values.shape), whole(outs.shape)],
        [whole(total), whole(values.shape)],
        [shape_of(*total), shape_of(*values.shape)],
        moved=8 * total[0] * HD,
        after=after,
    )(keys, values, outs)


def shards_square(
    residual,
    grad_out,
    norm_gain,
    w_gate,
    w_up,
    w_down,
    w_out,
    queries,
    attn_out,
    log_sum_exp,
    key_cache,
    value_cache,
):
    square = lax.axis_size("ctx")
    planes = lax.axis_size("wide") // 2
    here = lax.axis_index("ctx")
    local_width, hidden = w_gate.shape
    width = local_width * square
    gain = norm_gain[None, :]
    places = jnp.arange(square, dtype=jnp.int32) ^ here
    chain = Chain()
    rows_rel, rows_again = arrange(places, residual, grad_out, square, chain)

    offsets = list(range(planes))
    orders = [(0, 2, 1, 3) if unit % 2 == 0 else (0, 1, 2, 3) for unit in range(planes)]
    sources, stacked, kept, sent, folded = {}, {}, {}, {}, {}
    done, from_second, from_first, from_far = {}, {}, {}, {}
    splits, own_sums, far_sums, normed_parts = {}, {}, {}, {}

    def begin(*units):
        results = partial_sums(
            [orders[unit] for unit in units],
            [sources[unit] for unit in units],
            gain,
            w_gate,
            w_up,
            w_down,
            chain,
        )
        for unit, (keep, send, rows) in zip(units, results):
            kept[unit], stacked[unit] = keep, rows
            sent[unit] = flip(send, "ctx", orders[unit][2])

    def half(unit):
        kept[unit], send = fold(kept[unit], sent[unit], chain)
        folded[unit] = flip(send, "ctx", orders[unit][1])

    def centre(unit):
        result = middle(width, kept[unit], folded[unit], chain)
        done[unit] = result
        from_second[unit] = flip(result, "ctx", orders[unit][1])
        from_first[unit] = flip(result, "ctx", orders[unit][2])
        from_far[unit] = flip(from_second[unit], "ctx", orders[unit][2])

    def close(unit):
        own_sums[unit], far_sum, splits[unit] = normed_sums(
            orders[unit],
            (done[unit], from_second[unit], from_first[unit], from_far[unit]),
            w_gate,
            w_up,
            chain,
        )
        far_sums[unit] = flip(far_sum, "wide", 1)

    def settle(unit):
        part = join(own_sums[unit], far_sums[unit], chain)
        offset = offsets[unit]
        normed_parts[unit] = flip(part, "wide", offset * 2) if offset else part

    rows, columns = queries.shape
    heads = columns // HD
    mine = lax.axis_index("wide")
    spots = [mine ^ (offset * 2 + far) for offset in offsets for far in range(2)]
    spots = (jnp.stack(spots) ^ (here * 2)).astype(jnp.int32)
    keys_own, values_own = key_cache[0], value_cache[0]
    key_count = keys_own.shape[0]
    context = key_count * square
    first_pos = jnp.reshape(context - rows * square + here * rows, (1,)).astype(jnp.int32)
    lse_rows = log_sum_exp.reshape(heads * rows, 1)

    def wide_rows(unit, own):
        own = ordered(own, *chain.links)
        sources[unit] = (own, flip(own, "wide", 1))

    sources[0] = (rows_rel, flip(rows_rel, "wide", 1))
    own = flip(rows_again, "wide", 2)
    sources[1] = (own, flip(own, "wide", 1))
    later = ordered(rows_again, own)
    arriving = {unit: flip(later, "wide", offsets[unit] * 2) for unit in (2, 3)}
    begin(0, 1)
    wide_rows(2, arriving[2])
    wide_rows(3, arriving[3])
    begin(2, 3)
    chain.wait(spots, first_pos, lse_rows)
    half(0)
    half(1)
    centre(0)
    centre(1)
    row_parts, grad_parts = collect([stacked[unit] for unit in range(planes)], chain)
    saved, values_own = save(keys_own, values_own, attn_out, chain)
    chain.wait(from_second[0], from_second[1])
    half(2)
    half(3)
    centre(2)
    chain.wait(from_second[2])
    centre(3)
    close(0)
    chain.wait(from_second[3])
    close(1)
    settle(0)
    close(2)
    settle(1)
    close(3)
    settle(2)
    settle(3)
    all_splits = [splits[unit] for unit in range(planes)]
    grad_w_gate = weight_grad(0, row_parts, all_splits, hidden, chain)
    parts = [normed_parts[unit] for unit in range(planes)]
    grad_resid = finish(places, rows_rel, gain, parts, square, chain)

    across = [flip(grad_resid, "wide", offset * 2) if offset else grad_resid for offset in offsets]
    keys_near = flip(saved, "ctx", 1)
    keys_side = flip(saved, "ctx", 2)
    values_side = flip(values_own, "ctx", 2)
    values_near = flip(values_own, "ctx", 1)
    keys = [saved, keys_near, keys_side, flip(keys_near, "ctx", 2)]
    values = [values_own, values_near, values_side, flip(values_side, "ctx", 1)]
    outs = [(item, key_count // (heads * rows)) for item in keys]

    grad_w_up = weight_grad(1, row_parts, all_splits, hidden, chain)
    blocks = []
    for own in across:
        own = ordered(own, *chain.links) if own is not grad_resid else own
        blocks += [own, flip(own, "wide", 1)]
    grad_w_down = weight_grad(2, grad_parts, all_splits, hidden, chain)
    *parts, resid_rows = attn_grad(spots, blocks, w_out, square, chain)
    d_attn = [flip(part, "ctx", rel) if rel else part for rel, part in enumerate(parts)]
    probs = probs_of(places, first_pos, queries, lse_rows, keys, key_count, chain)
    grad_w_out = out_weight_grad(outs, resid_rows, heads, chain)
    grad_queries = attend(probs, attn_out, d_attn, keys, values, key_count, chain)
    return (grad_w_gate, grad_w_up, grad_w_down, grad_w_out, grad_resid, grad_queries)


def shards(*arrays):
    residual, queries, key_cache, w_gate = arrays[0], arrays[7], arrays[10], arrays[3]
    wide, ctx = lax.axis_size("wide"), lax.axis_size("ctx")
    planes = wide // 2
    heads = queries.shape[1] // HD
    fits = (
        ctx == 4
        and wide == KVH
        and planes == ctx
        and residual.shape[0] % 32 == 0
        and queries.shape[0] % 16 == 0
        and all(extent % TILE == 0 for extent in w_gate.shape + (queries.shape[1],))
        and key_cache.shape[1] % (heads * queries.shape[0]) == 0
    )
    return shards_square(*arrays) if fits else shards_general(*arrays)


def swapped(block, axis, bit):
    count = lax.axis_size(axis)
    route = []
    for low in range(count):
        high = low | 1 << bit
        if high != low and high < count:
            route += [(low, high), (high, low)]
    return lax.ppermute(block, axis, route)


def matmul(left, right):
    return jnp.dot(left, right, precision=highest, preferred_element_type=jnp.float32)


def matmul_tn(left, right):
    return lax.dot_general(
        left, right, (((0,), (0,)), ((), ())), precision=highest, preferred_element_type=jnp.float32
    )


def matmul_nt(left, right):
    return lax.dot_general(
        left, right, (((1,), (1,)), ((), ())), precision=highest, preferred_element_type=jnp.float32
    )


def join_group(own_part, far_part, upper):
    joined = []
    for own_item, far_item, join_dim in zip(own_part, far_part, (1, 1, 0, 0)):
        lower_first = jnp.concatenate((own_item, far_item), axis=join_dim)
        upper_first = jnp.concatenate((far_item, own_item), axis=join_dim)
        joined.append(jnp.where(upper, upper_first, lower_first))
    return tuple(joined)


def halve_group(partial_sums, member, split):
    for bit_index in reversed(range(split.bit_length() - 1)):
        half_width = partial_sums.shape[1] // 2
        upper = member // (1 << bit_index) % 2 == 1
        lower_half = partial_sums[:, :half_width]
        upper_half = partial_sums[:, half_width:]
        kept_half = jnp.where(upper, upper_half, lower_half)
        sent_half = jnp.where(upper, lower_half, upper_half)
        partial_sums = kept_half + swapped(sent_half, "wide", bit_index)
    return partial_sums


def shards_general(
    residual,
    grad_out,
    norm_gain,
    w_gate,
    w_up,
    w_down,
    w_out,
    queries,
    attn_out,
    log_sum_exp,
    key_cache,
    value_cache,
):
    width = residual.shape[1] * lax.axis_size("ctx")
    all_resid, all_grad = (
        lax.all_gather(residual, "wide", axis=0, tiled=True),
        lax.all_gather(grad_out, "wide", axis=0, tiled=True),
    )
    gained = all_resid * norm_gain[None, :]
    gate_raw, up_raw, d_hidden, squares = lax.psum(
        (
            matmul(gained, w_gate),
            matmul(gained, w_up),
            matmul_nt(all_grad, w_down),
            jnp.sum(all_resid * all_resid, axis=1),
        ),
        "ctx",
    )
    inv_rms = lax.rsqrt(squares / width + epsilon)
    normed = gained * inv_rms[:, None]
    gate_out = gate_raw * inv_rms[:, None]
    up_out = up_raw * inv_rms[:, None]
    sigmoid_gate = jax.nn.sigmoid(gate_out)
    activated = gate_out * sigmoid_gate
    hidden = activated * up_out
    grad_w_down = matmul_tn(hidden, all_grad)
    d_up = d_hidden * activated
    d_gate = d_hidden * up_out * sigmoid_gate * (1.0 + gate_out * (1.0 - sigmoid_gate))
    grad_w_gate = matmul_tn(normed, d_gate)
    grad_w_up = matmul_tn(normed, d_up)
    own_rows = residual.shape[0]
    d_normed = lax.psum_scatter(
        matmul_nt(d_gate, w_gate) + matmul_nt(d_up, w_up), "wide", scatter_dimension=0, tiled=True
    )
    scaled = d_normed * norm_gain[None, :]
    row_dot = lax.psum(jnp.sum(residual * scaled, axis=1), "ctx")
    own_inv = lax.dynamic_slice_in_dim(inv_rms, lax.axis_index("wide") * own_rows, own_rows, 0)
    cubed = own_inv * own_inv * own_inv
    grad_resid = (
        grad_out + own_inv[:, None] * scaled - residual * (cubed * row_dot / width)[:, None]
    )
    gathered_resid = lax.all_gather(grad_resid, "wide", axis=0, tiled=True)
    d_attn = lax.psum_scatter(
        matmul_nt(gathered_resid, w_out), "ctx", scatter_dimension=0, tiled=True
    )
    all_queries, all_outputs, all_dattn, all_lse = (
        lax.all_gather(queries, "ctx", axis=0, tiled=True),
        lax.all_gather(attn_out, "ctx", axis=0, tiled=True),
        lax.all_gather(d_attn, "ctx", axis=0, tiled=True),
        lax.all_gather(log_sum_exp, "ctx", axis=1, tiled=True),
    )
    grad_w_out = matmul_tn(all_outputs, gathered_resid)
    rows_total = all_queries.shape[0]
    head_dim = HD
    local_heads = all_queries.shape[1] // head_dim
    delta = jnp.sum((all_dattn * all_outputs).reshape(rows_total, local_heads, head_dim), axis=2).T
    split = lax.axis_size("wide") // KVH
    member = lax.axis_index("wide") % split
    group = (all_queries, all_dattn, all_lse, delta)
    for bit_index in range(split.bit_length() - 1):
        partner = swapped(group, "wide", bit_index)
        upper = member // (1 << bit_index) % 2 == 1
        group = join_group(group, partner, upper)
    group_queries, group_dattn, group_lse, group_delta = group
    group_count = group_queries.shape[1] // head_dim
    query_rows = (
        group_queries.reshape(rows_total, group_count, head_dim)
        .transpose(1, 0, 2)
        .reshape(group_count * rows_total, head_dim)
    )
    dout_rows = (
        group_dattn.reshape(rows_total, group_count, head_dim)
        .transpose(1, 0, 2)
        .reshape(group_count * rows_total, head_dim)
    )
    lse_rows = group_lse.reshape(group_count * rows_total)
    delta_rows = group_delta.reshape(group_count * rows_total)
    keys_local = key_cache[0]
    values_local = value_cache[0]
    key_count = keys_local.shape[0]
    ctx_count = lax.axis_size("ctx")
    context = key_count * ctx_count * split
    key_base = member * (key_count * ctx_count) + lax.axis_index("ctx") * key_count
    query_pos = jnp.tile(jnp.arange(rows_total, dtype=jnp.int32), group_count) + (
        context - rows_total
    )
    scale = 1.0 / math.sqrt(head_dim)
    block = min(512, key_count)
    accum = jnp.zeros((group_count * rows_total, head_dim), jnp.float32)
    for block_index in range(key_count // block):
        key_block = keys_local[block_index * block : (block_index + 1) * block]
        value_block = values_local[block_index * block : (block_index + 1) * block]
        key_pos = key_base + block_index * block + jnp.arange(block, dtype=jnp.int32)
        scores = matmul_nt(query_rows, key_block) * scale
        probs = jnp.where(
            key_pos[None, :] <= query_pos[:, None], jnp.exp(scores - lse_rows[:, None]), 0.0
        )
        dprobs = matmul_nt(dout_rows, value_block)
        accum = accum + matmul(probs * (dprobs - delta_rows[:, None]), key_block)
    dq_group = (
        (accum * scale)
        .reshape(group_count, rows_total, head_dim)
        .transpose(1, 0, 2)
        .reshape(rows_total, group_count * head_dim)
    )
    summed = lax.psum_scatter(dq_group, "ctx", scatter_dimension=0, tiled=True)
    grad_queries = halve_group(summed, member, split)
    return (grad_w_gate, grad_w_up, grad_w_down, grad_w_out, grad_resid, grad_queries)


def solution(mesh):
    placed = (
        P("wide", "ctx"),
        P("wide", "ctx"),
        P("ctx"),
        P("ctx", "wide"),
        P("ctx", "wide"),
        P("wide", "ctx"),
        P("wide", "ctx"),
        P("ctx", "wide"),
        P("ctx", "wide"),
        P("wide", "ctx"),
        P("wide", "ctx", None),
        P("wide", "ctx", None),
    )
    return jax.shard_map(
        shards,
        mesh=mesh,
        in_specs=placed,
        out_specs=(
            P("ctx", "wide"),
            P("ctx", "wide"),
            P("wide", "ctx"),
            P("wide", "ctx"),
            P("wide", "ctx"),
            P("ctx", "wide"),
        ),
        check_vma=False,
    )
```

```python
import functools
import math

import jax
import jax.numpy as jnp
from jax import lax
from jax.experimental import pallas as pl
from jax.experimental.pallas import tpu as pltpu
from jax.sharding import PartitionSpec as P

KVH = 8
HD = 128


epsilon = 1e-05
highest = lax.Precision.HIGHEST
f32 = jnp.float32
bf16 = jnp.bfloat16
LANES = 128
TILE = 256
VMEM_LIMIT = 16 * 1024 * 1024
VMEM_MOST = 60 * 1024 * 1024
NN = (((1,), (0,)), ((), ()))
NT = (((1,), (1,)), ((), ()))
TN = (((0,), (0,)), ((), ()))


def flip(block, axis, mask):
    count = lax.axis_size(axis)
    return lax.ppermute(block, axis, [(at, at ^ mask) for at in range(count)])


def pieces(values):
    high = values.astype(bf16)
    return high, (values - high.astype(f32)).astype(bf16)


def dot(left, right, dims):
    return lax.dot_general(left, right, dims, preferred_element_type=f32)


def dot3(left, right, dims):
    left_high, left_low = left
    right_high, right_low = right
    return (
        dot(left_high, right_high, dims)
        + dot(left_low, right_high, dims)
        + dot(left_high, right_low, dims)
    )


class Chain:
    def __init__(self):
        self.links = []

    def wait(self, *arrays):
        self.links += arrays


def call(
    name,
    kernel,
    grid,
    in_specs,
    out_specs,
    out_shape,
    scratch=(),
    flops=0,
    moved=0,
    after=None,
    limit=VMEM_LIMIT,
):
    count, waits, outs = len(in_specs), len(after.links), len(out_specs)

    def body(*refs):
        link = refs[count + waits + outs]
        link[...] = jnp.zeros_like(link)
        kernel(*refs[:count], *refs[count + waits : count + waits + outs], *refs[count + waits + outs + 1 :])

    run = pl.pallas_call(
        body,
        name=name,
        grid=grid,
        in_specs=list(in_specs) + [pl.BlockSpec(memory_space=pl.ANY)] * waits,
        out_specs=list(out_specs) + [whole((8, LANES))],
        out_shape=list(out_shape) + [shape_of(8, LANES)],
        scratch_shapes=list(scratch),
        compiler_params=pltpu.CompilerParams(vmem_limit_bytes=limit),
        cost_estimate=pl.CostEstimate(flops=4 * flops, bytes_accessed=4 * moved, transcendentals=0),
    )

    def apply(*operands):
        *results, link = run(*operands, *after.links)
        after.links = [link]
        return results if len(results) > 1 else results[0]

    return apply


def ordered(array, *earlier):
    anywhere = pl.BlockSpec(memory_space=pl.ANY)
    return pl.pallas_call(
        lambda *refs: None,
        name="ordered",
        in_specs=[anywhere] * (1 + len(earlier)),
        out_specs=anywhere,
        out_shape=jax.ShapeDtypeStruct(array.shape, array.dtype),
        input_output_aliases={0: 0},
    )(array, *earlier)


def whole(shape):
    return pl.BlockSpec(shape, lambda *_: (0,) * len(shape))


def shape_of(*shape, dtype=f32):
    return jax.ShapeDtypeStruct(shape, dtype)


def partial_kernel(orders, *refs):
    units = len(orders)
    sources = refs[: 2 * units]
    gain, w_gate, w_up, w_down = refs[2 * units : 2 * units + 4]
    results = refs[2 * units + 4 : -2]
    x_parts, g_parts = refs[-2:]
    step = pl.program_id(0)
    width = gain.shape[1]
    count = results[2].shape[0]
    total = units * count
    hidden = (results[0].shape[1] - LANES) // 3

    @pl.when(step == 0)
    def _():
        for unit, order in enumerate(orders):
            own, far = sources[2 * unit : 2 * unit + 2]
            keep, send, rows = results[3 * unit : 3 * unit + 3]
            cut = count // len(order)
            for at, rel in enumerate(order):
                piece = pl.ds(rel * cut // 2, cut // 2)
                rows[pl.ds(at * cut, cut // 2), :] = own[piece, :]
                rows[pl.ds(at * cut + cut // 2, cut // 2), :] = far[piece, :]
            resid = rows[:, :width]
            squares = jnp.broadcast_to(
                jnp.sum(resid * resid, axis=1, keepdims=True), (count, LANES)
            )
            keep[:, pl.ds(3 * hidden, LANES)] = squares[: count // 2]
            send[:, pl.ds(3 * hidden, LANES)] = squares[count // 2 :]
            gained = resid * gain[...]
            rows[:, :width] = gained
            for parts, values in ((x_parts, gained), (g_parts, rows[:, width:])):
                high, low = pieces(values)
                parts[pl.ds(unit * count, count), :] = high
                parts[pl.ds(total + unit * count, count), :] = low

    at = pl.multiple_of(step * TILE, TILE)
    for section, parts, weight, dims in (
        (0, x_parts, w_gate, NN),
        (1, x_parts, w_up, NN),
        (2, g_parts, w_down, NT),
    ):
        high, low = pieces(weight[...])
        both = dot(parts[...], high, dims)
        value = both[:total] + both[total:] + dot(parts[:total, :], low, dims)
        place = pl.ds(section * hidden + at, TILE)
        for unit in range(units):
            keep, send = results[3 * unit : 3 * unit + 2]
            start = unit * count
            keep[:, place] = value[start : start + count // 2]
            send[:, place] = value[start + count // 2 : start + count]


def partial_sums(orders, sources, gain, w_gate, w_up, w_down, after):
    width, hidden = w_gate.shape
    own_shape = sources[0][0].shape
    count = 2 * own_shape[0]
    total = count * len(orders)
    half = (count // 2, 3 * hidden + LANES)
    both = (count, 2 * width)
    flat = [item for pair in sources for item in pair]
    results = call(
        "partial",
        functools.partial(partial_kernel, orders),
        (hidden // TILE,),
        [whole(own_shape)] * len(flat)
        + [
            whole((1, width)),
            pl.BlockSpec((width, TILE), lambda j: (0, j)),
            pl.BlockSpec((width, TILE), lambda j: (0, j)),
            pl.BlockSpec((TILE, width), lambda j: (j, 0)),
        ],
        [whole(half), whole(half), whole(both)] * len(orders),
        [shape_of(*half), shape_of(*half), shape_of(*both)] * len(orders),
        [pltpu.VMEM((2 * total, width), bf16), pltpu.VMEM((2 * total, width), bf16)],
        flops=18 * total * width * hidden,
        moved=12 * width * hidden,
        after=after,
        limit=VMEM_MOST,
    )(*flat, gain, w_gate, w_up, w_down)
    return [results[3 * unit : 3 * unit + 3] for unit in range(len(orders))]


def fold_kernel(kept, got, keep, send):
    half = keep.shape[0]
    keep[...] = kept[:half, :] + got[:half, :]
    send[...] = kept[half:, :] + got[half:, :]


def fold(kept, got, after):
    rows, columns = kept.shape
    half = (rows // 2, columns)
    return call(
        "fold",
        fold_kernel,
        (1,),
        [whole(kept.shape)] * 2,
        [whole(half)] * 2,
        [shape_of(*half)] * 2,
        flops=rows * columns,
        moved=12 * rows * columns,
        after=after,
    )(kept, got)


def join_kernel(one, other, out):
    out[...] = one[...] + other[...]


def join(one, other, after):
    return call(
        "join",
        join_kernel,
        (1,),
        [whole(one.shape)] * 2,
        [whole(one.shape)],
        [shape_of(*one.shape)],
        moved=12 * one.size,
        after=after,
    )(one, other)


def middle_kernel(width, kept, got, out):
    hidden = (out.shape[1] - LANES) // 3
    gate_at, up_at, down_at = (pl.ds(part * hidden, hidden) for part in range(3))
    rest = pl.ds(3 * hidden, LANES)
    squares = (kept[:, rest] + got[:, rest])[:, :1]
    inv_rms = lax.rsqrt(squares / width + epsilon)
    gate_raw = kept[:, gate_at] + got[:, gate_at]
    up_raw = kept[:, up_at] + got[:, up_at]
    d_hidden = kept[:, down_at] + got[:, down_at]
    gate_out = gate_raw * inv_rms
    up_out = up_raw * inv_rms
    sigmoid_gate = jax.nn.sigmoid(gate_out)
    activated = gate_out * sigmoid_gate
    d_up = d_hidden * activated * inv_rms
    d_gate = d_hidden * up_out * sigmoid_gate * (1.0 + gate_out * (1.0 - sigmoid_gate)) * inv_rms
    out[:, gate_at] = d_gate
    out[:, up_at] = d_up
    out[:, down_at] = activated * up_out
    row_sum = jnp.sum(d_gate * gate_raw + d_up * up_raw, axis=1, keepdims=True)
    out[:, rest] = jnp.broadcast_to(row_sum * (inv_rms * inv_rms / width), (out.shape[0], LANES))


def middle(width, kept, got, after):
    rows, columns = kept.shape
    return call(
        "middle",
        functools.partial(middle_kernel, float(width)),
        (1,),
        [whole(kept.shape)] * 2,
        [whole(kept.shape)],
        [shape_of(rows, columns)],
        flops=20 * rows * columns,
        moved=12 * rows * columns,
        after=after,
    )(kept, got)


def normed_kernel(order, *refs):
    blocks = refs[: len(order)]
    w_gate, w_up, own, far, split, parts = refs[len(order) :]
    step = pl.program_id(0)
    cut = blocks[0].shape[0]
    count = cut * len(order)
    hidden = w_gate.shape[1]
    width = own.shape[1] - LANES

    @pl.when(step == 0)
    def _():
        for at, block in enumerate(blocks):
            high, low = pieces(block[:, : 3 * hidden])
            split[0, pl.ds(at * cut, cut), :] = high
            split[1, pl.ds(at * cut, cut), :] = low
            for section in range(2):
                columns = slice(section * hidden, (section + 1) * hidden)
                parts[section, pl.ds(at * cut, cut), :] = high[:, columns]
                parts[section, pl.ds(count + at * cut, cut), :] = low[:, columns]
            terms = block[:, pl.ds(3 * hidden, LANES)]
            piece = pl.ds(order[at] * cut // 2, cut // 2)
            own[piece, pl.ds(width, LANES)] = terms[: cut // 2]
            far[piece, pl.ds(width, LANES)] = terms[cut // 2 :]

    total = jnp.zeros((count, TILE), f32)
    for section, weight in ((0, w_gate), (1, w_up)):
        high, low = pieces(weight[...])
        both = dot(parts[section], high, NT)
        total += both[:count] + both[count:] + dot(parts[section, :count, :], low, NT)
    place = pl.ds(pl.multiple_of(step * TILE, TILE), TILE)
    for at, rel in enumerate(order):
        piece = pl.ds(rel * cut // 2, cut // 2)
        own[piece, place] = total[at * cut : at * cut + cut // 2]
        far[piece, place] = total[at * cut + cut // 2 : (at + 1) * cut]


def normed_sums(order, blocks, w_gate, w_up, after):
    width, hidden = w_gate.shape
    cut = blocks[0].shape[0]
    count = cut * len(order)
    half = (count // 2, width + LANES)
    weight = pl.BlockSpec((TILE, hidden), lambda j: (j, 0))
    return call(
        "normed",
        functools.partial(normed_kernel, order),
        (width // TILE,),
        [whole(blocks[0].shape)] * len(order) + [weight, weight],
        [whole(half), whole(half), whole((2, count, 3 * hidden))],
        [shape_of(*half), shape_of(*half), shape_of(2, count, 3 * hidden, dtype=bf16)],
        [pltpu.VMEM((2, 2 * count, hidden), bf16)],
        flops=12 * count * width * hidden,
        moved=8 * width * hidden,
        after=after,
    )(*blocks, w_gate, w_up)


def collect_kernel(*refs):
    rows, left, right = refs[:-2], refs[-2], refs[-1]
    width = right.shape[1]
    gained = jnp.concatenate([item[:, :width] for item in rows], axis=0)
    total = gained.shape[0]
    high, low = pieces(gained.T)
    left[:, :total] = high
    left[:, total : 2 * total] = low
    left[:, 2 * total :] = high
    high, low = pieces(jnp.concatenate([item[:, width:] for item in rows], axis=0))
    right[:total, :] = high
    right[total : 2 * total, :] = high
    right[2 * total :, :] = low


def collect(rows, after):
    total, width = sum(item.shape[0] for item in rows), rows[0].shape[1] // 2
    return call(
        "collect",
        collect_kernel,
        (1,),
        [whole(item.shape) for item in rows],
        [whole((width, 3 * total)), whole((3 * total, width))],
        [shape_of(width, 3 * total, dtype=bf16), shape_of(3 * total, width, dtype=bf16)],
        moved=16 * total * width,
        after=after,
        limit=VMEM_MOST,
    )(*rows)


def weight_kernel(flipped, rows, *refs):
    splits, out, whole_split = refs[:-2], refs[-2], refs[-1]
    count = splits[0].shape[1]
    total = count * len(splits)

    @pl.when(pl.program_id(0) == 0)
    def _():
        for at, split in enumerate(splits):
            for place, part in enumerate((0, 1, 0) if flipped else (0, 0, 1)):
                whole_split[pl.ds(place * total + at * count, count), :] = split[part]

    if flipped:
        begin = pl.multiple_of(pl.program_id(0) * out.shape[0], TILE)
        out[...] = dot(whole_split[:, pl.ds(begin, out.shape[0])], rows[...], TN)
    else:
        out[...] = dot(rows[...], whole_split[...], NN)


def weight_grad(section, rows, splits, hidden, after):
    flipped = section == 2
    total, width = rows.shape if flipped else rows.shape[::-1]
    if flipped:
        block = TILE
        out_shape = (hidden, width)
        row_spec = whole(rows.shape)
    else:
        block = 2 * TILE if width % (2 * TILE) == 0 else TILE
        out_shape = (width, hidden)
        row_spec = pl.BlockSpec((block, total), lambda j: (j, 0))
    return call(
        "weight",
        functools.partial(weight_kernel, flipped),
        (out_shape[0] // block,),
        [row_spec]
        + [
            pl.BlockSpec((2, split.shape[1], hidden), lambda j: (0, 0, section))
            for split in splits
        ],
        [pl.BlockSpec((block, out_shape[1]), lambda j: (j, 0))],
        [shape_of(*out_shape)],
        [pltpu.VMEM((total, hidden), bf16)],
        flops=2 * total * width * hidden,
        moved=4 * width * hidden,
        after=after,
        limit=VMEM_MOST,
    )(rows, *splits)


def by_head(source, heads):
    return jnp.concatenate([source[:, at * HD : (at + 1) * HD] for at in range(heads)], axis=0)


def probs_kernel(heads, scale, place, first, queries, lse, keys, *refs):
    rest, probs = refs[:-1], refs[-1]
    rows = queries.shape[0]
    query_rows = by_head(queries, heads)
    shift = lse[...]
    row_at = lax.broadcasted_iota(jnp.int32, (heads * rows, 1), 0)
    row_pos = lax.rem(row_at, rows) + first[0]
    for at, source in enumerate((keys,) + rest):
        key_count = source.shape[0]
        for begin in range(0, key_count, TILE):
            scores = lax.dot_general(
                query_rows,
                source[pl.ds(begin, TILE), :],
                NT,
                precision=highest,
                preferred_element_type=f32,
            )
            key_at = lax.broadcasted_iota(jnp.int32, (1, TILE), 1)
            key_pos = key_at + (place[at] * key_count + begin)
            probs[:, pl.ds(at * key_count + begin, TILE)] = jnp.where(
                key_pos <= row_pos, jnp.exp(scores * scale - shift), 0.0
            )


def probs_of(place, first, queries, lse, keys, key_count, after):
    rows, columns = queries.shape
    heads = columns // HD
    scalar = pl.BlockSpec(memory_space=pltpu.SMEM)
    total = (heads * rows, key_count * len(keys))
    return call(
        "probs",
        functools.partial(probs_kernel, heads, 1.0 / math.sqrt(HD)),
        (1,),
        [scalar, scalar, whole(queries.shape), whole(lse.shape)]
        + [pl.BlockSpec((key_count, HD), lambda i: (0, 0))] * len(keys),
        [whole(total)],
        [shape_of(*total)],
        flops=12 * rows * columns * total[1],
        moved=4 * total[0] * total[1],
        after=after,
    )(place, first, queries, lse, *keys)


def attend_kernel(heads, scale, probs, last_probs, outs, *refs):
    out = refs[-1]
    count = (len(refs) - 1) // 3
    douts, keys, values = refs[:count], refs[count : 2 * count], refs[2 * count : 3 * count]
    rows = outs.shape[0]
    dout = douts[0][...]
    for other in douts[1:]:
        dout = dout + other[...]
    dout_rows = by_head(dout, heads)
    delta = jnp.sum(dout_rows * by_head(outs, heads), axis=1, keepdims=True)
    dout_parts = pieces(dout_rows)
    total = jnp.zeros((heads * rows, HD), f32)
    for at in range(count):
        key_count = keys[at].shape[0]
        for begin in range(0, key_count, TILE):
            part = pl.ds(begin, TILE)
            dprobs = dot3(dout_parts, pieces(values[at][part, :]), NT)
            if at < count - 1:
                seen = probs[:, pl.ds(at * key_count + begin, TILE)]
            else:
                seen = last_probs[:, part]
            weights = seen * (dprobs - delta)
            total += dot3(pieces(weights), pieces(keys[at][part, :]), NN)
    for head in range(heads):
        out[:, head * HD : (head + 1) * HD] = total[head * rows : (head + 1) * rows] * scale


def attend(probs, last_probs, outs, douts, keys, values, key_count, after):
    rows, columns = outs.shape
    block = pl.BlockSpec((key_count, HD), lambda i: (0, 0))
    return call(
        "attend",
        functools.partial(attend_kernel, columns // HD, 1.0 / math.sqrt(HD)),
        (1,),
        [whole(probs.shape), whole(last_probs.shape), whole(outs.shape)]
        + [whole(outs.shape)] * len(douts)
        + [block] * (len(keys) + len(values)),
        [whole(outs.shape)],
        [shape_of(rows, columns)],
        flops=12 * rows * columns * key_count * len(keys),
        moved=4 * (probs.size + 2 * key_count * HD * len(keys)),
        after=after,
    )(probs, last_probs, outs, *douts, *keys, *values)


def attn_grad_kernel(blocks, place, weight, *refs):
    sources, outs = refs[:blocks], refs[blocks:-2]
    rel_rows, parts = refs[-2:]
    cut = outs[0].shape[0]
    total = cut * len(outs)
    piece = total // blocks

    @pl.when(pl.program_id(0) == 0)
    def _():
        for at, source in enumerate(sources):
            high, low = pieces(source[...])
            start = pl.multiple_of(place[at] * piece, piece)
            rel_rows[pl.ds(start, piece), :] = source[...]
            parts[pl.ds(start, piece), :] = high
            parts[pl.ds(pl.multiple_of(total + start, piece), piece), :] = low

    high, low = pieces(weight[...])
    both = dot(parts[...], high, NT)
    result = both[:total] + both[total:] + dot(parts[:total, :], low, NT)
    for at, out in enumerate(outs):
        out[...] = result[at * cut : (at + 1) * cut]


def attn_grad(place, sources, weight, count, after):
    piece, width = sources[0].shape
    total = piece * len(sources)
    columns = weight.shape[0]
    part = (total // count, columns)
    return call(
        "attn_grad",
        functools.partial(attn_grad_kernel, len(sources)),
        (columns // TILE,),
        [pl.BlockSpec(memory_space=pltpu.SMEM), pl.BlockSpec((TILE, width), lambda j: (j, 0))]
        + [whole(source.shape) for source in sources],
        [pl.BlockSpec((part[0], TILE), lambda j: (0, j))] * count + [whole((total, width))],
        [shape_of(*part)] * count + [shape_of(total, width)],
        [pltpu.VMEM((2 * total, width), bf16)],
        flops=6 * total * width * columns,
        moved=4 * width * columns,
        after=after,
    )(place, weight, *sources)


def out_weight_kernel(*refs):
    outs, (resid, grad) = refs[:-2], refs[-2:]
    rows = resid.shape[0] // len(outs)
    head = pl.ds(pl.multiple_of(pl.program_id(0) * rows, rows), rows)
    left = jnp.concatenate([out[head, :] for out in outs], axis=0)
    grad[...] = dot3(pieces(left), pieces(resid[...]), TN)


def out_weight_grad(outs, resid, heads, after):
    total, width = resid.shape
    return call(
        "out_weight",
        out_weight_kernel,
        (heads,),
        [pl.BlockSpec((heads * total // len(outs), HD), lambda j, at=at: (at, 0)) for _, at in outs]
        + [whole(resid.shape)],
        [pl.BlockSpec((HD, width), lambda j: (j, 0))],
        [shape_of(heads * HD, width)],
        flops=6 * total * width * heads * HD,
        moved=4 * width * heads * HD,
        after=after,
    )(*[item for item, _ in outs], resid)


def arrange_kernel(count, place, resid, grad, out, again):
    rows, width = resid.shape
    cut = rows // count
    for rel in range(count):
        source = pl.ds(pl.multiple_of(place[rel] * cut, cut), cut)
        out[pl.ds(rel * cut, cut), :width] = resid[source, :]
        out[pl.ds(rel * cut, cut), width:] = grad[source, :]
    again[...] = out[...]


def arrange(place, resid, grad, count, after):
    rows, width = resid.shape
    return call(
        "arrange",
        functools.partial(arrange_kernel, count),
        (1,),
        [pl.BlockSpec(memory_space=pltpu.SMEM)] + [whole(resid.shape)] * 2,
        [whole((rows, 2 * width))] * 2,
        [shape_of(rows, 2 * width)] * 2,
        moved=16 * rows * width,
        after=after,
        limit=VMEM_MOST,
    )(place, resid, grad)


def finish_kernel(count, place, rows_rel, gain, *refs):
    parts, out = refs[:-1], refs[-1]
    rows, width = out.shape
    cut = rows // count
    total = parts[0][...]
    for part in parts[1:]:
        total = total + part[...]
    result = (
        rows_rel[:, width:]
        + gain[...] * total[:, :width]
        - rows_rel[:, :width] * total[:, width : width + 1]
    )
    for rel in range(count):
        target = pl.ds(pl.multiple_of(place[rel] * cut, cut), cut)
        out[target, :] = result[rel * cut : (rel + 1) * cut]


def finish(place, rows_rel, gain, parts, count, after):
    rows, width = rows_rel.shape[0], gain.shape[1]
    return call(
        "finish",
        functools.partial(finish_kernel, count),
        (1,),
        [pl.BlockSpec(memory_space=pltpu.SMEM), whole(rows_rel.shape), whole(gain.shape)]
        + [whole(part.shape) for part in parts],
        [whole((rows, width))],
        [shape_of(rows, width)],
        moved=4 * rows * width * (len(parts) + 3),
        after=after,
    )(place, rows_rel, gain, *parts)


def save_kernel(heads, keys, outs, saved):
    count = keys.shape[0]
    rows = outs.shape[0]
    saved[pl.ds(0, count), :] = keys[...]
    for head in range(heads):
        saved[pl.ds(count + head * rows, rows), :] = outs[:, head * HD : (head + 1) * HD]


def save(keys, outs, after):
    count, rows, columns = keys.shape[0], outs.shape[0], outs.shape[1]
    heads = columns // HD
    total = (count + heads * rows, HD)
    return call(
        "save",
        functools.partial(save_kernel, heads),
        (1,),
        [whole(keys.shape), whole(outs.shape)],
        [whole(total)],
        [shape_of(*total)],
        moved=8 * total[0] * HD,
        after=after,
        limit=VMEM_MOST,
    )(keys, outs)


def shards_square(
    residual,
    grad_out,
    norm_gain,
    w_gate,
    w_up,
    w_down,
    w_out,
    queries,
    attn_out,
    log_sum_exp,
    key_cache,
    value_cache,
):
    square = lax.axis_size("ctx")
    planes = lax.axis_size("wide") // 2
    here = lax.axis_index("ctx")
    local_width, hidden = w_gate.shape
    width = local_width * square
    gain = norm_gain[None, :]
    places = jnp.arange(square, dtype=jnp.int32) ^ here
    chain = Chain()
    rows_rel, rows_again = arrange(places, residual, grad_out, square, chain)

    offsets = list(range(planes))
    orders = [(0, 2, 1, 3) if unit % 2 == 0 else (0, 1, 2, 3) for unit in range(planes)]
    sources, stacked, kept, sent, folded = {}, {}, {}, {}, {}
    done, from_second, from_first, from_far = {}, {}, {}, {}
    splits, own_sums, far_sums, normed_parts = {}, {}, {}, {}

    def begin(*units):
        results = partial_sums(
            [orders[unit] for unit in units],
            [sources[unit] for unit in units],
            gain,
            w_gate,
            w_up,
            w_down,
            chain,
        )
        for unit, (keep, send, rows) in zip(units, results):
            kept[unit], stacked[unit] = keep, rows
            sent[unit] = flip(send, "ctx", orders[unit][2])

    def half(unit):
        kept[unit], send = fold(kept[unit], sent[unit], chain)
        folded[unit] = flip(send, "ctx", orders[unit][1])

    def centre(unit):
        result = middle(width, kept[unit], folded[unit], chain)
        done[unit] = result
        from_second[unit] = flip(result, "ctx", orders[unit][1])
        from_first[unit] = flip(result, "ctx", orders[unit][2])
        from_far[unit] = flip(from_second[unit], "ctx", orders[unit][2])

    def close(unit):
        own_sums[unit], far_sum, splits[unit] = normed_sums(
            orders[unit],
            (done[unit], from_second[unit], from_first[unit], from_far[unit]),
            w_gate,
            w_up,
            chain,
        )
        far_sums[unit] = flip(far_sum, "wide", 1)

    def settle(unit):
        part = join(own_sums[unit], far_sums[unit], chain)
        offset = offsets[unit]
        normed_parts[unit] = flip(part, "wide", offset * 2) if offset else part

    rows, columns = queries.shape
    heads = columns // HD
    mine = lax.axis_index("wide")
    spots = [mine ^ (offset * 2 + far) for offset in offsets for far in range(2)]
    spots = (jnp.stack(spots) ^ (here * 2)).astype(jnp.int32)
    keys_own, values_own = key_cache[0], value_cache[0]
    key_count = keys_own.shape[0]
    context = key_count * square
    first_pos = jnp.reshape(context - rows * square + here * rows, (1,)).astype(jnp.int32)
    lse_rows = log_sum_exp.reshape(heads * rows, 1)

    def wide_rows(unit, own):
        own = ordered(own, *chain.links)
        sources[unit] = (own, flip(own, "wide", 1))

    sources[0] = (rows_rel, flip(rows_rel, "wide", 1))
    own = flip(rows_again, "wide", 2)
    sources[1] = (own, flip(own, "wide", 1))
    later = ordered(rows_again, own)
    arriving = {unit: flip(later, "wide", offsets[unit] * 2) for unit in (2, 3)}
    saved = save(keys_own, attn_out, chain)
    keys_near = flip(saved, "ctx", 1)
    keys_side = flip(saved, "ctx", 2)
    keys = [saved, keys_near, keys_side, flip(keys_near, "ctx", 2)]
    outs = [(item, key_count // (heads * rows)) for item in keys]
    begin(0, 1)
    chain.wait(keys_near, keys_side)
    wide_rows(2, arriving[2])
    wide_rows(3, arriving[3])
    begin(2, 3)
    chain.wait(spots, first_pos, lse_rows)
    half(0)
    half(1)
    row_parts, grad_parts = collect([stacked[unit] for unit in range(planes)], chain)
    centre(0)
    centre(1)
    half(2)
    half(3)
    probs = probs_of(
        places[:-1], first_pos, queries, lse_rows, keys[:-1], key_count, chain
    )
    chain.wait(from_second[0], from_second[1])
    centre(2)
    chain.wait(from_second[2])
    centre(3)
    close(0)
    chain.wait(from_second[3])
    close(1)
    settle(0)
    close(2)
    settle(1)
    close(3)
    settle(2)
    settle(3)
    values_side = flip(values_own, "ctx", 2)
    values_near = flip(values_own, "ctx", 1)
    values = [values_own, values_near, values_side, flip(values_side, "ctx", 1)]
    all_splits = [splits[unit] for unit in range(planes)]
    grad_w_gate = weight_grad(0, row_parts, all_splits, hidden, chain)
    parts = [normed_parts[unit] for unit in range(planes)]
    grad_resid = finish(places, rows_rel, gain, parts, square, chain)

    across = [flip(grad_resid, "wide", offset * 2) if offset else grad_resid for offset in offsets]
    chain.wait(values_near, values_side)
    grad_w_up = weight_grad(1, row_parts, all_splits, hidden, chain)
    blocks = []
    for own in across:
        own = ordered(own, *chain.links) if own is not grad_resid else own
        blocks += [own, flip(own, "wide", 1)]
    grad_w_down = weight_grad(2, grad_parts, all_splits, hidden, chain)
    chain.wait(values[3], keys[3])
    *parts, resid_rows = attn_grad(spots, blocks, w_out, square, chain)
    d_attn = [flip(part, "ctx", rel) if rel else part for rel, part in enumerate(parts)]
    last_probs = probs_of(
        places[-1:], first_pos, queries, lse_rows, keys[-1:], key_count, chain
    )
    grad_w_out = out_weight_grad(outs, resid_rows, heads, chain)
    grad_queries = attend(probs, last_probs, attn_out, d_attn, keys, values, key_count, chain)
    return (grad_w_gate, grad_w_up, grad_w_down, grad_w_out, grad_resid, grad_queries)


def shards(*arrays):
    residual, queries, key_cache, w_gate = arrays[0], arrays[7], arrays[10], arrays[3]
    wide, ctx = lax.axis_size("wide"), lax.axis_size("ctx")
    planes = wide // 2
    heads = queries.shape[1] // HD
    fits = (
        ctx == 4
        and wide == KVH
        and planes == ctx
        and residual.shape[0] % 32 == 0
        and queries.shape[0] % 16 == 0
        and all(extent % TILE == 0 for extent in w_gate.shape + (queries.shape[1],))
        and key_cache.shape[1] % (heads * queries.shape[0]) == 0
    )
    return shards_square(*arrays) if fits else shards_general(*arrays)


def swapped(block, axis, bit):
    count = lax.axis_size(axis)
    route = []
    for low in range(count):
        high = low | 1 << bit
        if high != low and high < count:
            route += [(low, high), (high, low)]
    return lax.ppermute(block, axis, route)


def matmul(left, right):
    return jnp.dot(left, right, precision=highest, preferred_element_type=jnp.float32)


def matmul_tn(left, right):
    return lax.dot_general(
        left, right, (((0,), (0,)), ((), ())), precision=highest, preferred_element_type=jnp.float32
    )


def matmul_nt(left, right):
    return lax.dot_general(
        left, right, (((1,), (1,)), ((), ())), precision=highest, preferred_element_type=jnp.float32
    )


def join_group(own_part, far_part, upper):
    joined = []
    for own_item, far_item, join_dim in zip(own_part, far_part, (1, 1, 0, 0)):
        lower_first = jnp.concatenate((own_item, far_item), axis=join_dim)
        upper_first = jnp.concatenate((far_item, own_item), axis=join_dim)
        joined.append(jnp.where(upper, upper_first, lower_first))
    return tuple(joined)


def halve_group(partial_sums, member, split):
    for bit_index in reversed(range(split.bit_length() - 1)):
        half_width = partial_sums.shape[1] // 2
        upper = member // (1 << bit_index) % 2 == 1
        lower_half = partial_sums[:, :half_width]
        upper_half = partial_sums[:, half_width:]
        kept_half = jnp.where(upper, upper_half, lower_half)
        sent_half = jnp.where(upper, lower_half, upper_half)
        partial_sums = kept_half + swapped(sent_half, "wide", bit_index)
    return partial_sums


def shards_general(
    residual,
    grad_out,
    norm_gain,
    w_gate,
    w_up,
    w_down,
    w_out,
    queries,
    attn_out,
    log_sum_exp,
    key_cache,
    value_cache,
):
    width = residual.shape[1] * lax.axis_size("ctx")
    all_resid, all_grad = (
        lax.all_gather(residual, "wide", axis=0, tiled=True),
        lax.all_gather(grad_out, "wide", axis=0, tiled=True),
    )
    gained = all_resid * norm_gain[None, :]
    gate_raw, up_raw, d_hidden, squares = lax.psum(
        (
            matmul(gained, w_gate),
            matmul(gained, w_up),
            matmul_nt(all_grad, w_down),
            jnp.sum(all_resid * all_resid, axis=1),
        ),
        "ctx",
    )
    inv_rms = lax.rsqrt(squares / width + epsilon)
    normed = gained * inv_rms[:, None]
    gate_out = gate_raw * inv_rms[:, None]
    up_out = up_raw * inv_rms[:, None]
    sigmoid_gate = jax.nn.sigmoid(gate_out)
    activated = gate_out * sigmoid_gate
    hidden = activated * up_out
    grad_w_down = matmul_tn(hidden, all_grad)
    d_up = d_hidden * activated
    d_gate = d_hidden * up_out * sigmoid_gate * (1.0 + gate_out * (1.0 - sigmoid_gate))
    grad_w_gate = matmul_tn(normed, d_gate)
    grad_w_up = matmul_tn(normed, d_up)
    own_rows = residual.shape[0]
    d_normed = lax.psum_scatter(
        matmul_nt(d_gate, w_gate) + matmul_nt(d_up, w_up), "wide", scatter_dimension=0, tiled=True
    )
    scaled = d_normed * norm_gain[None, :]
    row_dot = lax.psum(jnp.sum(residual * scaled, axis=1), "ctx")
    own_inv = lax.dynamic_slice_in_dim(inv_rms, lax.axis_index("wide") * own_rows, own_rows, 0)
    cubed = own_inv * own_inv * own_inv
    grad_resid = (
        grad_out + own_inv[:, None] * scaled - residual * (cubed * row_dot / width)[:, None]
    )
    gathered_resid = lax.all_gather(grad_resid, "wide", axis=0, tiled=True)
    d_attn = lax.psum_scatter(
        matmul_nt(gathered_resid, w_out), "ctx", scatter_dimension=0, tiled=True
    )
    all_queries, all_outputs, all_dattn, all_lse = (
        lax.all_gather(queries, "ctx", axis=0, tiled=True),
        lax.all_gather(attn_out, "ctx", axis=0, tiled=True),
        lax.all_gather(d_attn, "ctx", axis=0, tiled=True),
        lax.all_gather(log_sum_exp, "ctx", axis=1, tiled=True),
    )
    grad_w_out = matmul_tn(all_outputs, gathered_resid)
    rows_total = all_queries.shape[0]
    head_dim = HD
    local_heads = all_queries.shape[1] // head_dim
    delta = jnp.sum((all_dattn * all_outputs).reshape(rows_total, local_heads, head_dim), axis=2).T
    split = lax.axis_size("wide") // KVH
    member = lax.axis_index("wide") % split
    group = (all_queries, all_dattn, all_lse, delta)
    for bit_index in range(split.bit_length() - 1):
        partner = swapped(group, "wide", bit_index)
        upper = member // (1 << bit_index) % 2 == 1
        group = join_group(group, partner, upper)
    group_queries, group_dattn, group_lse, group_delta = group
    group_count = group_queries.shape[1] // head_dim
    query_rows = (
        group_queries.reshape(rows_total, group_count, head_dim)
        .transpose(1, 0, 2)
        .reshape(group_count * rows_total, head_dim)
    )
    dout_rows = (
        group_dattn.reshape(rows_total, group_count, head_dim)
        .transpose(1, 0, 2)
        .reshape(group_count * rows_total, head_dim)
    )
    lse_rows = group_lse.reshape(group_count * rows_total)
    delta_rows = group_delta.reshape(group_count * rows_total)
    keys_local = key_cache[0]
    values_local = value_cache[0]
    key_count = keys_local.shape[0]
    ctx_count = lax.axis_size("ctx")
    context = key_count * ctx_count * split
    key_base = member * (key_count * ctx_count) + lax.axis_index("ctx") * key_count
    query_pos = jnp.tile(jnp.arange(rows_total, dtype=jnp.int32), group_count) + (
        context - rows_total
    )
    scale = 1.0 / math.sqrt(head_dim)
    block = min(512, key_count)
    accum = jnp.zeros((group_count * rows_total, head_dim), jnp.float32)
    for block_index in range(key_count // block):
        key_block = keys_local[block_index * block : (block_index + 1) * block]
        value_block = values_local[block_index * block : (block_index + 1) * block]
        key_pos = key_base + block_index * block + jnp.arange(block, dtype=jnp.int32)
        scores = matmul_nt(query_rows, key_block) * scale
        probs = jnp.where(
            key_pos[None, :] <= query_pos[:, None], jnp.exp(scores - lse_rows[:, None]), 0.0
        )
        dprobs = matmul_nt(dout_rows, value_block)
        accum = accum + matmul(probs * (dprobs - delta_rows[:, None]), key_block)
    dq_group = (
        (accum * scale)
        .reshape(group_count, rows_total, head_dim)
        .transpose(1, 0, 2)
        .reshape(rows_total, group_count * head_dim)
    )
    summed = lax.psum_scatter(dq_group, "ctx", scatter_dimension=0, tiled=True)
    grad_queries = halve_group(summed, member, split)
    return (grad_w_gate, grad_w_up, grad_w_down, grad_w_out, grad_resid, grad_queries)


def solution(mesh):
    placed = (
        P("wide", "ctx"),
        P("wide", "ctx"),
        P("ctx"),
        P("ctx", "wide"),
        P("ctx", "wide"),
        P("wide", "ctx"),
        P("wide", "ctx"),
        P("ctx", "wide"),
        P("ctx", "wide"),
        P("wide", "ctx"),
        P("wide", "ctx", None),
        P("wide", "ctx", None),
    )
    return jax.shard_map(
        shards,
        mesh=mesh,
        in_specs=placed,
        out_specs=(
            P("ctx", "wide"),
            P("ctx", "wide"),
            P("wide", "ctx"),
            P("wide", "ctx"),
            P("wide", "ctx"),
            P("ctx", "wide"),
        ),
        check_vma=False,
    )
```

```python
import functools
import math

import jax
import jax.numpy as jnp
from jax import lax
from jax.experimental import pallas as pl
from jax.experimental.pallas import tpu as pltpu
from jax.sharding import PartitionSpec as P

KVH = 8
HD = 128


epsilon = 1e-05
highest = lax.Precision.HIGHEST
f32 = jnp.float32
bf16 = jnp.bfloat16
LANES = 128
TILE = 256
VMEM_LIMIT = 16 * 1024 * 1024
VMEM_MOST = 60 * 1024 * 1024
NN = (((1,), (0,)), ((), ()))
NT = (((1,), (1,)), ((), ()))
TN = (((0,), (0,)), ((), ()))


def flip(block, axis, mask):
    count = lax.axis_size(axis)
    return lax.ppermute(block, axis, [(at, at ^ mask) for at in range(count)])


def pieces(values):
    high = values.astype(bf16)
    return high, (values - high.astype(f32)).astype(bf16)


def dot(left, right, dims):
    return lax.dot_general(left, right, dims, preferred_element_type=f32)


def dot3(left, right, dims):
    left_high, left_low = left
    right_high, right_low = right
    return (
        dot(left_high, right_high, dims)
        + dot(left_low, right_high, dims)
        + dot(left_high, right_low, dims)
    )


class Chain:
    def __init__(self):
        self.links = []

    def wait(self, *arrays):
        self.links += arrays


def call(
    name,
    kernel,
    grid,
    in_specs,
    out_specs,
    out_shape,
    scratch=(),
    flops=0,
    moved=0,
    after=None,
    limit=VMEM_LIMIT,
):
    count, waits, outs = len(in_specs), len(after.links), len(out_specs)

    def body(*refs):
        link = refs[count + waits + outs]
        link[...] = jnp.zeros_like(link)
        kernel(*refs[:count], *refs[count + waits : count + waits + outs], *refs[count + waits + outs + 1 :])

    run = pl.pallas_call(
        body,
        name=name,
        grid=grid,
        in_specs=list(in_specs) + [pl.BlockSpec(memory_space=pl.ANY)] * waits,
        out_specs=list(out_specs) + [whole((8, LANES))],
        out_shape=list(out_shape) + [shape_of(8, LANES)],
        scratch_shapes=list(scratch),
        compiler_params=pltpu.CompilerParams(vmem_limit_bytes=limit),
        cost_estimate=pl.CostEstimate(flops=4 * flops, bytes_accessed=4 * moved, transcendentals=0),
    )

    def apply(*operands):
        *results, link = run(*operands, *after.links)
        after.links = [link]
        return results if len(results) > 1 else results[0]

    return apply


def ordered(array, *earlier):
    anywhere = pl.BlockSpec(memory_space=pl.ANY)
    return pl.pallas_call(
        lambda *refs: None,
        name="ordered",
        in_specs=[anywhere] * (1 + len(earlier)),
        out_specs=anywhere,
        out_shape=jax.ShapeDtypeStruct(array.shape, array.dtype),
        input_output_aliases={0: 0},
    )(array, *earlier)


def whole(shape):
    return pl.BlockSpec(shape, lambda *_: (0,) * len(shape))


def shape_of(*shape, dtype=f32):
    return jax.ShapeDtypeStruct(shape, dtype)


def partial_kernel(orders, *refs):
    units = len(orders)
    sources = refs[: 2 * units]
    gain, w_gate, w_up, w_down = refs[2 * units : 2 * units + 4]
    results = refs[2 * units + 4 : -2]
    x_parts, g_parts = refs[-2:]
    step = pl.program_id(0)
    width = gain.shape[1]
    count = results[2].shape[0]
    total = units * count
    hidden = (results[0].shape[1] - LANES) // 3

    @pl.when(step == 0)
    def _():
        for unit, order in enumerate(orders):
            own, far = sources[2 * unit : 2 * unit + 2]
            keep, send, rows = results[3 * unit : 3 * unit + 3]
            cut = count // len(order)
            for at, rel in enumerate(order):
                piece = pl.ds(rel * cut // 2, cut // 2)
                rows[pl.ds(at * cut, cut // 2), :] = own[piece, :]
                rows[pl.ds(at * cut + cut // 2, cut // 2), :] = far[piece, :]
            resid = rows[:, :width]
            squares = jnp.broadcast_to(
                jnp.sum(resid * resid, axis=1, keepdims=True), (count, LANES)
            )
            keep[:, pl.ds(3 * hidden, LANES)] = squares[: count // 2]
            send[:, pl.ds(3 * hidden, LANES)] = squares[count // 2 :]
            gained = resid * gain[...]
            rows[:, :width] = gained
            for parts, values in ((x_parts, gained), (g_parts, rows[:, width:])):
                high, low = pieces(values)
                parts[pl.ds(unit * count, count), :] = high
                parts[pl.ds(total + unit * count, count), :] = low

    at = pl.multiple_of(step * TILE, TILE)
    for section, parts, weight, dims in (
        (0, x_parts, w_gate, NN),
        (1, x_parts, w_up, NN),
        (2, g_parts, w_down, NT),
    ):
        high, low = pieces(weight[...])
        both = dot(parts[...], high, dims)
        value = both[:total] + both[total:] + dot(parts[:total, :], low, dims)
        place = pl.ds(section * hidden + at, TILE)
        for unit in range(units):
            keep, send = results[3 * unit : 3 * unit + 2]
            start = unit * count
            keep[:, place] = value[start : start + count // 2]
            send[:, place] = value[start + count // 2 : start + count]


def partial_sums(orders, sources, gain, w_gate, w_up, w_down, after):
    width, hidden = w_gate.shape
    own_shape = sources[0][0].shape
    count = 2 * own_shape[0]
    total = count * len(orders)
    half = (count // 2, 3 * hidden + LANES)
    both = (count, 2 * width)
    flat = [item for pair in sources for item in pair]
    results = call(
        "partial",
        functools.partial(partial_kernel, orders),
        (hidden // TILE,),
        [whole(own_shape)] * len(flat)
        + [
            whole((1, width)),
            pl.BlockSpec((width, TILE), lambda j: (0, j)),
            pl.BlockSpec((width, TILE), lambda j: (0, j)),
            pl.BlockSpec((TILE, width), lambda j: (j, 0)),
        ],
        [whole(half), whole(half), whole(both)] * len(orders),
        [shape_of(*half), shape_of(*half), shape_of(*both)] * len(orders),
        [pltpu.VMEM((2 * total, width), bf16), pltpu.VMEM((2 * total, width), bf16)],
        flops=18 * total * width * hidden,
        moved=12 * width * hidden,
        after=after,
        limit=VMEM_MOST,
    )(*flat, gain, w_gate, w_up, w_down)
    return [results[3 * unit : 3 * unit + 3] for unit in range(len(orders))]


def fold_kernel(kept, got, keep, send):
    half = keep.shape[0]
    keep[...] = kept[:half, :] + got[:half, :]
    send[...] = kept[half:, :] + got[half:, :]


def fold(kept, got, after):
    rows, columns = kept.shape
    half = (rows // 2, columns)
    return call(
        "fold",
        fold_kernel,
        (1,),
        [whole(kept.shape)] * 2,
        [whole(half)] * 2,
        [shape_of(*half)] * 2,
        flops=rows * columns,
        moved=12 * rows * columns,
        after=after,
    )(kept, got)


def join_kernel(one, other, out):
    out[...] = one[...] + other[...]


def join(one, other, after):
    return call(
        "join",
        join_kernel,
        (1,),
        [whole(one.shape)] * 2,
        [whole(one.shape)],
        [shape_of(*one.shape)],
        moved=12 * one.size,
        after=after,
    )(one, other)


def middle_kernel(width, kept, got, out):
    hidden = (out.shape[1] - LANES) // 3
    gate_at, up_at, down_at = (pl.ds(part * hidden, hidden) for part in range(3))
    rest = pl.ds(3 * hidden, LANES)
    squares = (kept[:, rest] + got[:, rest])[:, :1]
    inv_rms = lax.rsqrt(squares / width + epsilon)
    gate_raw = kept[:, gate_at] + got[:, gate_at]
    up_raw = kept[:, up_at] + got[:, up_at]
    d_hidden = kept[:, down_at] + got[:, down_at]
    gate_out = gate_raw * inv_rms
    up_out = up_raw * inv_rms
    sigmoid_gate = jax.nn.sigmoid(gate_out)
    activated = gate_out * sigmoid_gate
    d_up = d_hidden * activated * inv_rms
    d_gate = d_hidden * up_out * sigmoid_gate * (1.0 + gate_out * (1.0 - sigmoid_gate)) * inv_rms
    out[:, gate_at] = d_gate
    out[:, up_at] = d_up
    out[:, down_at] = activated * up_out
    row_sum = jnp.sum(d_gate * gate_raw + d_up * up_raw, axis=1, keepdims=True)
    out[:, rest] = jnp.broadcast_to(row_sum * (inv_rms * inv_rms / width), (out.shape[0], LANES))


def middle(width, kept, got, after):
    rows, columns = kept.shape
    return call(
        "middle",
        functools.partial(middle_kernel, float(width)),
        (1,),
        [whole(kept.shape)] * 2,
        [whole(kept.shape)],
        [shape_of(rows, columns)],
        flops=20 * rows * columns,
        moved=12 * rows * columns,
        after=after,
    )(kept, got)


def normed_kernel(order, *refs):
    blocks = refs[: len(order)]
    w_gate, w_up, own, far, split, parts = refs[len(order) :]
    step = pl.program_id(0)
    cut = blocks[0].shape[0]
    count = cut * len(order)
    hidden = w_gate.shape[1]
    width = own.shape[1] - LANES

    @pl.when(step == 0)
    def _():
        for at, block in enumerate(blocks):
            high, low = pieces(block[:, : 3 * hidden])
            split[0, pl.ds(at * cut, cut), :] = high
            split[1, pl.ds(at * cut, cut), :] = low
            for section in range(2):
                columns = slice(section * hidden, (section + 1) * hidden)
                parts[section, pl.ds(at * cut, cut), :] = high[:, columns]
                parts[section, pl.ds(count + at * cut, cut), :] = low[:, columns]
            terms = block[:, pl.ds(3 * hidden, LANES)]
            piece = pl.ds(order[at] * cut // 2, cut // 2)
            own[piece, pl.ds(width, LANES)] = terms[: cut // 2]
            far[piece, pl.ds(width, LANES)] = terms[cut // 2 :]

    total = jnp.zeros((count, TILE), f32)
    for section, weight in ((0, w_gate), (1, w_up)):
        high, low = pieces(weight[...])
        both = dot(parts[section], high, NT)
        total += both[:count] + both[count:] + dot(parts[section, :count, :], low, NT)
    place = pl.ds(pl.multiple_of(step * TILE, TILE), TILE)
    for at, rel in enumerate(order):
        piece = pl.ds(rel * cut // 2, cut // 2)
        own[piece, place] = total[at * cut : at * cut + cut // 2]
        far[piece, place] = total[at * cut + cut // 2 : (at + 1) * cut]


def normed_sums(order, blocks, w_gate, w_up, after):
    width, hidden = w_gate.shape
    cut = blocks[0].shape[0]
    count = cut * len(order)
    half = (count // 2, width + LANES)
    weight = pl.BlockSpec((TILE, hidden), lambda j: (j, 0))
    return call(
        "normed",
        functools.partial(normed_kernel, order),
        (width // TILE,),
        [whole(blocks[0].shape)] * len(order) + [weight, weight],
        [whole(half), whole(half), whole((2, count, 3 * hidden))],
        [shape_of(*half), shape_of(*half), shape_of(2, count, 3 * hidden, dtype=bf16)],
        [pltpu.VMEM((2, 2 * count, hidden), bf16)],
        flops=12 * count * width * hidden,
        moved=8 * width * hidden,
        after=after,
    )(*blocks, w_gate, w_up)


def collect_kernel(*refs):
    rows, left, right = refs[:-2], refs[-2], refs[-1]
    width = right.shape[1]
    gained = jnp.concatenate([item[:, :width] for item in rows], axis=0)
    total = gained.shape[0]
    high, low = pieces(gained.T)
    left[:, :total] = high
    left[:, total : 2 * total] = low
    left[:, 2 * total :] = high
    high, low = pieces(jnp.concatenate([item[:, width:] for item in rows], axis=0))
    right[:total, :] = high
    right[total : 2 * total, :] = high
    right[2 * total :, :] = low


def collect(rows, after):
    total, width = sum(item.shape[0] for item in rows), rows[0].shape[1] // 2
    return call(
        "collect",
        collect_kernel,
        (1,),
        [whole(item.shape) for item in rows],
        [whole((width, 3 * total)), whole((3 * total, width))],
        [shape_of(width, 3 * total, dtype=bf16), shape_of(3 * total, width, dtype=bf16)],
        moved=16 * total * width,
        after=after,
        limit=VMEM_MOST,
    )(*rows)


def weight_kernel(flipped, rows, *refs):
    splits, out, whole_split = refs[:-2], refs[-2], refs[-1]
    count = splits[0].shape[1]
    total = count * len(splits)

    @pl.when(pl.program_id(0) == 0)
    def _():
        for at, split in enumerate(splits):
            for place, part in enumerate((0, 1, 0) if flipped else (0, 0, 1)):
                whole_split[pl.ds(place * total + at * count, count), :] = split[part]

    if flipped:
        begin = pl.multiple_of(pl.program_id(0) * out.shape[0], LANES)
        out[...] = dot(whole_split[:, pl.ds(begin, out.shape[0])], rows[...], TN)
    else:
        out[...] = dot(rows[...], whole_split[...], NN)


def weight_grad(section, rows, splits, hidden, after):
    flipped = section == 2
    total, width = rows.shape if flipped else rows.shape[::-1]
    if flipped:
        block = hidden // 2 if hidden % (2 * LANES) == 0 else TILE
        out_shape = (hidden, width)
        row_spec = whole(rows.shape)
    else:
        block = 2 * TILE if width % (2 * TILE) == 0 else TILE
        out_shape = (width, hidden)
        row_spec = pl.BlockSpec((block, total), lambda j: (j, 0))
    return call(
        "weight",
        functools.partial(weight_kernel, flipped),
        (out_shape[0] // block,),
        [row_spec]
        + [
            pl.BlockSpec((2, split.shape[1], hidden), lambda j: (0, 0, section))
            for split in splits
        ],
        [pl.BlockSpec((block, out_shape[1]), lambda j: (j, 0))],
        [shape_of(*out_shape)],
        [pltpu.VMEM((total, hidden), bf16)],
        flops=2 * total * width * hidden,
        moved=4 * width * hidden,
        after=after,
        limit=VMEM_MOST,
    )(rows, *splits)


def by_head(source, heads):
    return jnp.concatenate([source[:, at * HD : (at + 1) * HD] for at in range(heads)], axis=0)


def probs_kernel(heads, scale, place, first, queries, lse, keys, *refs):
    rest, probs = refs[:-1], refs[-1]
    rows = queries.shape[0]
    query_rows = by_head(queries, heads)
    shift = lse[...]
    row_at = lax.broadcasted_iota(jnp.int32, (heads * rows, 1), 0)
    row_pos = lax.rem(row_at, rows) + first[0]
    for at, source in enumerate((keys,) + rest):
        key_count = source.shape[0]
        for begin in range(0, key_count, TILE):
            scores = lax.dot_general(
                query_rows,
                source[pl.ds(begin, TILE), :],
                NT,
                precision=highest,
                preferred_element_type=f32,
            )
            key_at = lax.broadcasted_iota(jnp.int32, (1, TILE), 1)
            key_pos = key_at + (place[at] * key_count + begin)
            probs[:, pl.ds(at * key_count + begin, TILE)] = jnp.where(
                key_pos <= row_pos, jnp.exp(scores * scale - shift), 0.0
            )


def probs_of(place, first, queries, lse, keys, key_count, after):
    rows, columns = queries.shape
    heads = columns // HD
    scalar = pl.BlockSpec(memory_space=pltpu.SMEM)
    total = (heads * rows, key_count * len(keys))
    return call(
        "probs",
        functools.partial(probs_kernel, heads, 1.0 / math.sqrt(HD)),
        (1,),
        [scalar, scalar, whole(queries.shape), whole(lse.shape)]
        + [pl.BlockSpec((key_count, HD), lambda i: (0, 0))] * len(keys),
        [whole(total)],
        [shape_of(*total)],
        flops=12 * rows * columns * total[1],
        moved=4 * total[0] * total[1],
        after=after,
    )(place, first, queries, lse, *keys)


def attend_kernel(heads, scale, probs, last_probs, outs, *refs):
    out = refs[-1]
    count = (len(refs) - 1) // 3
    douts, keys, values = refs[:count], refs[count : 2 * count], refs[2 * count : 3 * count]
    rows = outs.shape[0]
    dout = douts[0][...]
    for other in douts[1:]:
        dout = dout + other[...]
    dout_rows = by_head(dout, heads)
    delta = jnp.sum(dout_rows * by_head(outs, heads), axis=1, keepdims=True)
    dout_parts = pieces(dout_rows)
    total = jnp.zeros((heads * rows, HD), f32)
    for at in range(count):
        key_count = keys[at].shape[0]
        for begin in range(0, key_count, TILE):
            part = pl.ds(begin, TILE)
            dprobs = dot3(dout_parts, pieces(values[at][part, :]), NT)
            if at < count - 1:
                seen = probs[:, pl.ds(at * key_count + begin, TILE)]
            else:
                seen = last_probs[:, part]
            weights = seen * (dprobs - delta)
            total += dot3(pieces(weights), pieces(keys[at][part, :]), NN)
    for head in range(heads):
        out[:, head * HD : (head + 1) * HD] = total[head * rows : (head + 1) * rows] * scale


def attend(probs, last_probs, outs, douts, keys, values, key_count, after):
    rows, columns = outs.shape
    block = pl.BlockSpec((key_count, HD), lambda i: (0, 0))
    return call(
        "attend",
        functools.partial(attend_kernel, columns // HD, 1.0 / math.sqrt(HD)),
        (1,),
        [whole(probs.shape), whole(last_probs.shape), whole(outs.shape)]
        + [whole(outs.shape)] * len(douts)
        + [block] * (len(keys) + len(values)),
        [whole(outs.shape)],
        [shape_of(rows, columns)],
        flops=12 * rows * columns * key_count * len(keys),
        moved=4 * (probs.size + 2 * key_count * HD * len(keys)),
        after=after,
    )(probs, last_probs, outs, *douts, *keys, *values)


def attn_grad_kernel(blocks, place, weight, *refs):
    sources, outs = refs[:blocks], refs[blocks:-2]
    rel_rows, parts = refs[-2:]
    cut = outs[0].shape[0]
    total = cut * len(outs)
    piece = total // blocks

    @pl.when(pl.program_id(0) == 0)
    def _():
        for at, source in enumerate(sources):
            high, low = pieces(source[...])
            start = pl.multiple_of(place[at] * piece, piece)
            rel_rows[pl.ds(start, piece), :] = source[...]
            parts[pl.ds(start, piece), :] = high
            parts[pl.ds(pl.multiple_of(total + start, piece), piece), :] = low

    high, low = pieces(weight[...])
    both = dot(parts[...], high, NT)
    result = both[:total] + both[total:] + dot(parts[:total, :], low, NT)
    for at, out in enumerate(outs):
        out[...] = result[at * cut : (at + 1) * cut]


def attn_grad(place, sources, weight, count, after):
    piece, width = sources[0].shape
    total = piece * len(sources)
    columns = weight.shape[0]
    part = (total // count, columns)
    return call(
        "attn_grad",
        functools.partial(attn_grad_kernel, len(sources)),
        (columns // TILE,),
        [pl.BlockSpec(memory_space=pltpu.SMEM), pl.BlockSpec((TILE, width), lambda j: (j, 0))]
        + [whole(source.shape) for source in sources],
        [pl.BlockSpec((part[0], TILE), lambda j: (0, j))] * count + [whole((total, width))],
        [shape_of(*part)] * count + [shape_of(total, width)],
        [pltpu.VMEM((2 * total, width), bf16)],
        flops=6 * total * width * columns,
        moved=4 * width * columns,
        after=after,
        limit=VMEM_MOST,
    )(place, weight, *sources)


def out_weight_kernel(*refs):
    outs, (resid, grad) = refs[:-2], refs[-2:]
    rows = resid.shape[0] // len(outs)
    head = pl.ds(pl.multiple_of(pl.program_id(0) * rows, rows), rows)
    left = jnp.concatenate([out[head, :] for out in outs], axis=0)
    grad[...] = dot3(pieces(left), pieces(resid[...]), TN)


def out_weight_grad(outs, resid, heads, after):
    total, width = resid.shape
    return call(
        "out_weight",
        out_weight_kernel,
        (heads,),
        [pl.BlockSpec((heads * total // len(outs), HD), lambda j, at=at: (at, 0)) for _, at in outs]
        + [whole(resid.shape)],
        [pl.BlockSpec((HD, width), lambda j: (j, 0))],
        [shape_of(heads * HD, width)],
        flops=6 * total * width * heads * HD,
        moved=4 * width * heads * HD,
        after=after,
    )(*[item for item, _ in outs], resid)


def arrange_kernel(count, place, resid, grad, out, again):
    rows, width = resid.shape
    cut = rows // count
    for rel in range(count):
        source = pl.ds(pl.multiple_of(place[rel] * cut, cut), cut)
        out[pl.ds(rel * cut, cut), :width] = resid[source, :]
        out[pl.ds(rel * cut, cut), width:] = grad[source, :]
    again[...] = out[...]


def arrange(place, resid, grad, count, after):
    rows, width = resid.shape
    return call(
        "arrange",
        functools.partial(arrange_kernel, count),
        (1,),
        [pl.BlockSpec(memory_space=pltpu.SMEM)] + [whole(resid.shape)] * 2,
        [whole((rows, 2 * width))] * 2,
        [shape_of(rows, 2 * width)] * 2,
        moved=16 * rows * width,
        after=after,
        limit=VMEM_MOST,
    )(place, resid, grad)


def finish_kernel(count, place, rows_rel, gain, *refs):
    parts, out = refs[:-1], refs[-1]
    rows, width = out.shape
    cut = rows // count
    total = parts[0][...]
    for part in parts[1:]:
        total = total + part[...]
    result = (
        rows_rel[:, width:]
        + gain[...] * total[:, :width]
        - rows_rel[:, :width] * total[:, width : width + 1]
    )
    for rel in range(count):
        target = pl.ds(pl.multiple_of(place[rel] * cut, cut), cut)
        out[target, :] = result[rel * cut : (rel + 1) * cut]


def finish(place, rows_rel, gain, parts, count, after):
    rows, width = rows_rel.shape[0], gain.shape[1]
    return call(
        "finish",
        functools.partial(finish_kernel, count),
        (1,),
        [pl.BlockSpec(memory_space=pltpu.SMEM), whole(rows_rel.shape), whole(gain.shape)]
        + [whole(part.shape) for part in parts],
        [whole((rows, width))],
        [shape_of(rows, width)],
        moved=4 * rows * width * (len(parts) + 3),
        after=after,
        limit=VMEM_MOST,
    )(place, rows_rel, gain, *parts)


def save_kernel(heads, keys, outs, saved):
    count = keys.shape[0]
    rows = outs.shape[0]
    saved[pl.ds(0, count), :] = keys[...]
    for head in range(heads):
        saved[pl.ds(count + head * rows, rows), :] = outs[:, head * HD : (head + 1) * HD]


def save(keys, outs, after):
    count, rows, columns = keys.shape[0], outs.shape[0], outs.shape[1]
    heads = columns // HD
    total = (count + heads * rows, HD)
    return call(
        "save",
        functools.partial(save_kernel, heads),
        (1,),
        [whole(keys.shape), whole(outs.shape)],
        [whole(total)],
        [shape_of(*total)],
        moved=8 * total[0] * HD,
        after=after,
        limit=VMEM_MOST,
    )(keys, outs)


def shards_square(
    residual,
    grad_out,
    norm_gain,
    w_gate,
    w_up,
    w_down,
    w_out,
    queries,
    attn_out,
    log_sum_exp,
    key_cache,
    value_cache,
):
    square = lax.axis_size("ctx")
    planes = lax.axis_size("wide") // 2
    here = lax.axis_index("ctx")
    local_width, hidden = w_gate.shape
    width = local_width * square
    gain = norm_gain[None, :]
    places = jnp.arange(square, dtype=jnp.int32) ^ here
    chain = Chain()
    rows_rel, rows_again = arrange(places, residual, grad_out, square, chain)

    offsets = list(range(planes))
    orders = [(0, 2, 1, 3) if unit % 2 == 0 else (0, 1, 2, 3) for unit in range(planes)]
    sources, stacked, kept, sent, folded = {}, {}, {}, {}, {}
    done, from_second, from_first, from_far = {}, {}, {}, {}
    splits, own_sums, far_sums, normed_parts = {}, {}, {}, {}

    def begin(*units):
        results = partial_sums(
            [orders[unit] for unit in units],
            [sources[unit] for unit in units],
            gain,
            w_gate,
            w_up,
            w_down,
            chain,
        )
        for unit, (keep, send, rows) in zip(units, results):
            kept[unit], stacked[unit] = keep, rows
            sent[unit] = flip(send, "ctx", orders[unit][2])

    def half(unit):
        kept[unit], send = fold(kept[unit], sent[unit], chain)
        folded[unit] = flip(send, "ctx", orders[unit][1])

    def centre(unit):
        result = middle(width, kept[unit], folded[unit], chain)
        done[unit] = result
        from_second[unit] = flip(result, "ctx", orders[unit][1])
        from_first[unit] = flip(result, "ctx", orders[unit][2])
        from_far[unit] = flip(from_second[unit], "ctx", orders[unit][2])

    def close(unit):
        own_sums[unit], far_sum, splits[unit] = normed_sums(
            orders[unit],
            (done[unit], from_second[unit], from_first[unit], from_far[unit]),
            w_gate,
            w_up,
            chain,
        )
        far_sums[unit] = flip(far_sum, "wide", 1)

    def settle(unit):
        part = join(own_sums[unit], far_sums[unit], chain)
        offset = offsets[unit]
        normed_parts[unit] = flip(part, "wide", offset * 2) if offset else part

    rows, columns = queries.shape
    heads = columns // HD
    mine = lax.axis_index("wide")
    spots = [mine ^ (offset * 2 + far) for offset in offsets for far in range(2)]
    spots = (jnp.stack(spots) ^ (here * 2)).astype(jnp.int32)
    keys_own, values_own = key_cache[0], value_cache[0]
    key_count = keys_own.shape[0]
    context = key_count * square
    first_pos = jnp.reshape(context - rows * square + here * rows, (1,)).astype(jnp.int32)
    lse_rows = log_sum_exp.reshape(heads * rows, 1)

    def wide_rows(unit, own):
        own = ordered(own, *chain.links)
        sources[unit] = (own, flip(own, "wide", 1))

    sources[0] = (rows_rel, flip(rows_rel, "wide", 1))
    saved = save(keys_own, attn_out, chain)
    own = ordered(flip(rows_again, "wide", 2), *chain.links)
    sources[1] = (own, flip(own, "wide", 1))
    later = ordered(rows_again, own)
    arriving = {unit: flip(later, "wide", offsets[unit] * 2) for unit in (2, 3)}
    keys_near = flip(saved, "ctx", 1)
    keys_side = flip(saved, "ctx", 2)
    keys = [saved, keys_near, keys_side, flip(keys_near, "ctx", 2)]
    outs = [(item, key_count // (heads * rows)) for item in keys]
    begin(0, 1)
    chain.wait(keys_near, keys_side)
    wide_rows(2, arriving[2])
    wide_rows(3, arriving[3])
    begin(2, 3)
    near_places, last_places = places[:-1], places[-1:]
    chain.wait(spots, first_pos, lse_rows, near_places, last_places)
    half(0)
    half(1)
    row_parts, grad_parts = collect([stacked[unit] for unit in range(planes)], chain)
    centre(0)
    centre(1)
    half(2)
    half(3)
    probs = probs_of(
        near_places, first_pos, queries, lse_rows, keys[:-1], key_count, chain
    )
    chain.wait(from_second[0], from_second[1])
    centre(2)
    chain.wait(from_second[2])
    centre(3)
    close(0)
    chain.wait(from_second[3])
    close(1)
    settle(0)
    close(2)
    settle(1)
    close(3)
    settle(2)
    settle(3)
    values_side = flip(values_own, "ctx", 2)
    values_near = flip(values_own, "ctx", 1)
    values = [values_own, values_near, values_side, flip(values_side, "ctx", 1)]
    all_splits = [splits[unit] for unit in range(planes)]
    grad_w_gate = weight_grad(0, row_parts, all_splits, hidden, chain)
    parts = [normed_parts[unit] for unit in range(planes)]
    grad_resid = finish(places, rows_rel, gain, parts, square, chain)

    across = [flip(grad_resid, "wide", offset * 2) if offset else grad_resid for offset in offsets]
    chain.wait(values_near, values_side)
    grad_w_up = weight_grad(1, row_parts, all_splits, hidden, chain)
    blocks = []
    for own in across:
        own = ordered(own, *chain.links) if own is not grad_resid else own
        blocks += [own, flip(own, "wide", 1)]
    grad_w_down = weight_grad(2, grad_parts, all_splits, hidden, chain)
    chain.wait(values[3], keys[3])
    *parts, resid_rows = attn_grad(spots, blocks, w_out, square, chain)
    d_attn = [flip(part, "ctx", rel) if rel else part for rel, part in enumerate(parts)]
    last_probs = probs_of(
        last_places, first_pos, queries, lse_rows, keys[-1:], key_count, chain
    )
    grad_w_out = out_weight_grad(outs, resid_rows, heads, chain)
    grad_queries = attend(probs, last_probs, attn_out, d_attn, keys, values, key_count, chain)
    return (grad_w_gate, grad_w_up, grad_w_down, grad_w_out, grad_resid, grad_queries)


def shards(*arrays):
    residual, queries, key_cache, w_gate = arrays[0], arrays[7], arrays[10], arrays[3]
    wide, ctx = lax.axis_size("wide"), lax.axis_size("ctx")
    planes = wide // 2
    heads = queries.shape[1] // HD
    fits = (
        ctx == 4
        and wide == KVH
        and planes == ctx
        and residual.shape[0] % 32 == 0
        and queries.shape[0] % 16 == 0
        and all(extent % TILE == 0 for extent in w_gate.shape + (queries.shape[1],))
        and key_cache.shape[1] % (heads * queries.shape[0]) == 0
    )
    return shards_square(*arrays) if fits else shards_general(*arrays)


def swapped(block, axis, bit):
    count = lax.axis_size(axis)
    route = []
    for low in range(count):
        high = low | 1 << bit
        if high != low and high < count:
            route += [(low, high), (high, low)]
    return lax.ppermute(block, axis, route)


def matmul(left, right):
    return jnp.dot(left, right, precision=highest, preferred_element_type=jnp.float32)


def matmul_tn(left, right):
    return lax.dot_general(
        left, right, (((0,), (0,)), ((), ())), precision=highest, preferred_element_type=jnp.float32
    )


def matmul_nt(left, right):
    return lax.dot_general(
        left, right, (((1,), (1,)), ((), ())), precision=highest, preferred_element_type=jnp.float32
    )


def join_group(own_part, far_part, upper):
    joined = []
    for own_item, far_item, join_dim in zip(own_part, far_part, (1, 1, 0, 0)):
        lower_first = jnp.concatenate((own_item, far_item), axis=join_dim)
        upper_first = jnp.concatenate((far_item, own_item), axis=join_dim)
        joined.append(jnp.where(upper, upper_first, lower_first))
    return tuple(joined)


def halve_group(partial_sums, member, split):
    for bit_index in reversed(range(split.bit_length() - 1)):
        half_width = partial_sums.shape[1] // 2
        upper = member // (1 << bit_index) % 2 == 1
        lower_half = partial_sums[:, :half_width]
        upper_half = partial_sums[:, half_width:]
        kept_half = jnp.where(upper, upper_half, lower_half)
        sent_half = jnp.where(upper, lower_half, upper_half)
        partial_sums = kept_half + swapped(sent_half, "wide", bit_index)
    return partial_sums


def shards_general(
    residual,
    grad_out,
    norm_gain,
    w_gate,
    w_up,
    w_down,
    w_out,
    queries,
    attn_out,
    log_sum_exp,
    key_cache,
    value_cache,
):
    width = residual.shape[1] * lax.axis_size("ctx")
    all_resid, all_grad = (
        lax.all_gather(residual, "wide", axis=0, tiled=True),
        lax.all_gather(grad_out, "wide", axis=0, tiled=True),
    )
    gained = all_resid * norm_gain[None, :]
    gate_raw, up_raw, d_hidden, squares = lax.psum(
        (
            matmul(gained, w_gate),
            matmul(gained, w_up),
            matmul_nt(all_grad, w_down),
            jnp.sum(all_resid * all_resid, axis=1),
        ),
        "ctx",
    )
    inv_rms = lax.rsqrt(squares / width + epsilon)
    normed = gained * inv_rms[:, None]
    gate_out = gate_raw * inv_rms[:, None]
    up_out = up_raw * inv_rms[:, None]
    sigmoid_gate = jax.nn.sigmoid(gate_out)
    activated = gate_out * sigmoid_gate
    hidden = activated * up_out
    grad_w_down = matmul_tn(hidden, all_grad)
    d_up = d_hidden * activated
    d_gate = d_hidden * up_out * sigmoid_gate * (1.0 + gate_out * (1.0 - sigmoid_gate))
    grad_w_gate = matmul_tn(normed, d_gate)
    grad_w_up = matmul_tn(normed, d_up)
    own_rows = residual.shape[0]
    d_normed = lax.psum_scatter(
        matmul_nt(d_gate, w_gate) + matmul_nt(d_up, w_up), "wide", scatter_dimension=0, tiled=True
    )
    scaled = d_normed * norm_gain[None, :]
    row_dot = lax.psum(jnp.sum(residual * scaled, axis=1), "ctx")
    own_inv = lax.dynamic_slice_in_dim(inv_rms, lax.axis_index("wide") * own_rows, own_rows, 0)
    cubed = own_inv * own_inv * own_inv
    grad_resid = (
        grad_out + own_inv[:, None] * scaled - residual * (cubed * row_dot / width)[:, None]
    )
    gathered_resid = lax.all_gather(grad_resid, "wide", axis=0, tiled=True)
    d_attn = lax.psum_scatter(
        matmul_nt(gathered_resid, w_out), "ctx", scatter_dimension=0, tiled=True
    )
    all_queries, all_outputs, all_dattn, all_lse = (
        lax.all_gather(queries, "ctx", axis=0, tiled=True),
        lax.all_gather(attn_out, "ctx", axis=0, tiled=True),
        lax.all_gather(d_attn, "ctx", axis=0, tiled=True),
        lax.all_gather(log_sum_exp, "ctx", axis=1, tiled=True),
    )
    grad_w_out = matmul_tn(all_outputs, gathered_resid)
    rows_total = all_queries.shape[0]
    head_dim = HD
    local_heads = all_queries.shape[1] // head_dim
    delta = jnp.sum((all_dattn * all_outputs).reshape(rows_total, local_heads, head_dim), axis=2).T
    split = lax.axis_size("wide") // KVH
    member = lax.axis_index("wide") % split
    group = (all_queries, all_dattn, all_lse, delta)
    for bit_index in range(split.bit_length() - 1):
        partner = swapped(group, "wide", bit_index)
        upper = member // (1 << bit_index) % 2 == 1
        group = join_group(group, partner, upper)
    group_queries, group_dattn, group_lse, group_delta = group
    group_count = group_queries.shape[1] // head_dim
    query_rows = (
        group_queries.reshape(rows_total, group_count, head_dim)
        .transpose(1, 0, 2)
        .reshape(group_count * rows_total, head_dim)
    )
    dout_rows = (
        group_dattn.reshape(rows_total, group_count, head_dim)
        .transpose(1, 0, 2)
        .reshape(group_count * rows_total, head_dim)
    )
    lse_rows = group_lse.reshape(group_count * rows_total)
    delta_rows = group_delta.reshape(group_count * rows_total)
    keys_local = key_cache[0]
    values_local = value_cache[0]
    key_count = keys_local.shape[0]
    ctx_count = lax.axis_size("ctx")
    context = key_count * ctx_count * split
    key_base = member * (key_count * ctx_count) + lax.axis_index("ctx") * key_count
    query_pos = jnp.tile(jnp.arange(rows_total, dtype=jnp.int32), group_count) + (
        context - rows_total
    )
    scale = 1.0 / math.sqrt(head_dim)
    block = min(512, key_count)
    accum = jnp.zeros((group_count * rows_total, head_dim), jnp.float32)
    for block_index in range(key_count // block):
        key_block = keys_local[block_index * block : (block_index + 1) * block]
        value_block = values_local[block_index * block : (block_index + 1) * block]
        key_pos = key_base + block_index * block + jnp.arange(block, dtype=jnp.int32)
        scores = matmul_nt(query_rows, key_block) * scale
        probs = jnp.where(
            key_pos[None, :] <= query_pos[:, None], jnp.exp(scores - lse_rows[:, None]), 0.0
        )
        dprobs = matmul_nt(dout_rows, value_block)
        accum = accum + matmul(probs * (dprobs - delta_rows[:, None]), key_block)
    dq_group = (
        (accum * scale)
        .reshape(group_count, rows_total, head_dim)
        .transpose(1, 0, 2)
        .reshape(rows_total, group_count * head_dim)
    )
    summed = lax.psum_scatter(dq_group, "ctx", scatter_dimension=0, tiled=True)
    grad_queries = halve_group(summed, member, split)
    return (grad_w_gate, grad_w_up, grad_w_down, grad_w_out, grad_resid, grad_queries)


def solution(mesh):
    placed = (
        P("wide", "ctx"),
        P("wide", "ctx"),
        P("ctx"),
        P("ctx", "wide"),
        P("ctx", "wide"),
        P("wide", "ctx"),
        P("wide", "ctx"),
        P("ctx", "wide"),
        P("ctx", "wide"),
        P("wide", "ctx"),
        P("wide", "ctx", None),
        P("wide", "ctx", None),
    )
    return jax.shard_map(
        shards,
        mesh=mesh,
        in_specs=placed,
        out_specs=(
            P("ctx", "wide"),
            P("ctx", "wide"),
            P("wide", "ctx"),
            P("wide", "ctx"),
            P("wide", "ctx"),
            P("ctx", "wide"),
        ),
        check_vma=False,
    )
```
